256 devices in a mesh: pipe: 16 (over z, core), tensor: 8 (over y, x_lo), dp: 2 (over x_hi).
Axes of the slice: x: 4 (x_hi: 2, x_lo: 2; x = x_hi * 2 + x_lo), y: 4, z: 8, core: 2. Of those that a mesh axis runs over, the one named last changes fastest.
Arguments:
- layer_input: bfloat16 [16384, 8192], P(('pipe', 'dp')), may hold values from -600 to 600
- norm_gain: float32 [8192], replicated, may hold values from 0.1 to 1.9
- w_query: bfloat16 [8192, 4096], P('pipe', 'tensor'), may hold values from -4 to 4
- w_kv: bfloat16 [8192, 1024], P('pipe', 'tensor'), may hold values from -4 to 4
- lengths: int32 [32, 4], P(('pipe', 'dp')), may hold values from 1 to 256, 512 in all within a row
- out_grad: bfloat16 [16384, 4096], P(('pipe', 'dp'), 'tensor'), may hold values from -6 to 6
Outputs:
- attn_out: bfloat16 [16384, 4096], P(('pipe', 'dp'), 'tensor')
- grad_query: float32 [8192, 4096], P(('pipe', 'dp'), 'tensor')
- grad_kv: float32 [8192, 1024], P(('pipe', 'dp'), 'tensor')
The draws below stay inside these ranges and needn't reach their ends.
Inputs may be any that keep to these rules, and one draw needn't show every extreme that they name: Each row holds the lengths of the 4 sequences of one micro-batch in order; they sum to 512.
All inputs are finite; a program needn't handle non-finite values.
Results may differ from the reference program's by a relative error of at most 0.0065.
The reference program's roundings to bfloat16 on the way (of `normed`, `query_act`, `kv_act`, `probs_bf`, `score_grad`, `grad_q` and `grad_kv_act`) count: a program that leaves them out, or rounds other values in their place, can miss the bound.
Values may be sent and summed in bfloat16 or wider, within the bound.
No kernel may reach another device: no remote copies, remote signals or barrier semaphores. Data moves between devices by JAX's collectives and lax.ppermute only.
A program may use at most 128 MiB of HBM per device.

```python
import math
import jax
import jax.numpy as jnp
import numpy as np
from jax import lax

D = 8192
HEADS = 32
KV_HEADS = 4
HD = 128
TOK_DEV = 512
DOCS = 4
MICRO = 32
TOKENS = 16384


def draw_layer_input(key, part):
    key = jax.random.fold_in(key, 11)
    key_main, key_rows, key_cols = jax.random.split(key, 3)
    row_scale = jnp.exp(jax.random.uniform(key_rows, (TOKENS, 1), jnp.float32) * math.log(10.0))
    col_scale = jnp.exp(jax.random.uniform(key_cols, (1, D), jnp.float32) * math.log(10.0))
    entries = jnp.clip(jax.random.normal(key_main, (TOKENS, D), jnp.float32), -6.0, 6.0)
    return (entries * row_scale * col_scale).astype(jnp.bfloat16)


def draw_w_query(key, part):
    key = jax.random.fold_in(key, 21)
    entries = jnp.clip(jax.random.normal(key, (D, HEADS, HD), jnp.float32), -6.0, 6.0) / math.sqrt(D)
    return entries.reshape(D, HEADS * HD).astype(jnp.bfloat16)


def draw_w_kv(key, part):
    key = jax.random.fold_in(key, 22)
    key_k, key_v = jax.random.split(key)
    key_part = jnp.clip(jax.random.normal(key_k, (D, KV_HEADS, HD), jnp.float32), -6.0, 6.0) / math.sqrt(D)
    value_part = jnp.clip(jax.random.normal(key_v, (D, KV_HEADS, HD), jnp.float32), -6.0, 6.0) / math.sqrt(D)
    joined = jnp.concatenate([key_part.reshape(D, KV_HEADS * HD), value_part.reshape(D, KV_HEADS * HD)], axis=1)
    return joined.astype(jnp.bfloat16)


def block_levels(stream_key, dims, cuts, least, top_value):
    def one(dim, blocks):
        draws = jax.random.uniform(jax.random.fold_in(jax.random.fold_in(stream_key, 6), dim), (blocks,), jnp.float32, least / len(cuts), top_value / len(cuts))
        return jnp.repeat(jnp.exp(draws), dims[dim] // blocks).reshape((-1,) + (1,) * (len(dims) - dim - 1))

    level = one(*cuts[0])
    for cut in cuts[1:]:
        level = level * one(*cut)
    return level


def length_profile(amount, total, most, skew):
    loads = [(1 << 20) // math.isqrt(grade ** skew) + 1 for grade in range(2, amount + 1)]
    rest, counts = total - most - (amount - 1), [1] * (amount - 1)
    while rest > 0:
        movable = [i for i in range(amount - 1) if counts[i] < most]
        mass, left = sum([loads[i] for i in movable]), rest
        for i in movable:
            addition = min(most - counts[i], max(1, left * loads[i] // mass), rest)
            counts[i] = counts[i] + addition
            rest = rest - addition
    return np.array([most] + counts)


def ragged(own_key, count, total, reach, skew):
    if count == 2:
        one = jax.random.randint(own_key, (), max(1, total - reach), min(reach, total - 1) + 1)
        return jnp.stack([one, total - one])
    sizes = jnp.asarray(length_profile(count, total, reach, skew), jnp.int32)
    pairs = (count - 1) // 2
    donor, sink = sizes[1:1 + 2 * pairs:2], sizes[2:2 + 2 * pairs:2]
    slack = jnp.minimum(donor - 1, reach - sink)
    passed = jax.random.randint(jax.random.fold_in(own_key, 1), (pairs,), 0, 1 << 20) % (slack + 1)
    sizes = sizes.at[1:1 + 2 * pairs:2].set(donor - passed).at[2:2 + 2 * pairs:2].set(sink + passed)
    return sizes[jax.random.permutation(jax.random.fold_in(own_key, 2), count)]


def gaussian(own_key, extent, width, reach, shards=(), held_as=jnp.bfloat16):
    values = width * jax.random.normal(own_key, extent, jnp.float32)
    if shards:
        values = values * block_levels(own_key, extent, shards, -0.22, 0.18)
    return jnp.clip(values, -reach, reach).astype(held_as)


def setup_inputs(seed: int = 0) -> dict:
    key_of = jax.random.split(jax.random.key(seed), 7)
    layer_input = draw_layer_input(jax.random.fold_in(key_of[6], 71), 0)
    norm_gain = jnp.clip(1.0 + 0.18 * jax.random.normal(key_of[1], (D,), jnp.float32), 0.1, 1.9)
    w_query = draw_w_query(jax.random.fold_in(key_of[6], 71), 0)
    w_kv = draw_w_kv(jax.random.fold_in(key_of[6], 71), 0)
    lengths = jax.vmap(lambda own: ragged(own, DOCS, TOK_DEV, TOK_DEV // 2, 2))(jax.random.split(key_of[4], MICRO)).reshape((MICRO, DOCS)).astype(jnp.int32)
    out_grad = gaussian(key_of[5], (TOKENS, HEADS * HD), 1.0, 6.0, ((0, 32), (1, 8)))
    return dict(layer_input=layer_input, norm_gain=norm_gain, w_query=w_query, w_kv=w_kv, lengths=lengths, out_grad=out_grad)


def allowed_pairs(seq_lengths, tok_count):
    position = jnp.arange(tok_count, dtype=jnp.int32)
    bounds = jnp.cumsum(seq_lengths).astype(jnp.int32)
    segment = lax.optimization_barrier(jnp.sum((position[:, None] >= bounds[None, :]).astype(jnp.int32), axis=1))
    return (segment[:, None] == segment[None, :]) & (position[None, :] <= position[:, None])

def attend(query_h, key_h, value_h, grad_out, seq_lengths):
    group_size = HEADS // KV_HEADS
    tok_count = query_h.shape[0]
    score_scale = query_h.shape[-1] ** (-0.5)
    keys_rep = jnp.repeat(key_h, group_size, axis=1).astype(jnp.float32)
    values_rep = jnp.repeat(value_h, group_size, axis=1).astype(jnp.float32)
    q_float = query_h.astype(jnp.float32)
    g_float = grad_out.astype(jnp.float32)
    allowed = allowed_pairs(seq_lengths, tok_count)
    scores = jnp.einsum('qhd,khd->hqk', q_float, keys_rep) * score_scale
    scores = jnp.where(allowed[None], scores, -1e+30)
    row_max = lax.optimization_barrier(jnp.max(scores, axis=-1, keepdims=True))
    weights_exp = jnp.exp(scores - row_max)
    probs = weights_exp / lax.optimization_barrier(jnp.sum(weights_exp, axis=-1, keepdims=True))
    probs_bf = probs.astype(jnp.bfloat16)
    attended = jnp.einsum('hqk,khd->qhd', probs_bf.astype(jnp.float32), values_rep).astype(jnp.bfloat16)
    back_scores = jnp.einsum('qhd,khd->hqk', g_float, values_rep)
    row_delta = lax.optimization_barrier(jnp.sum(probs * back_scores, axis=-1, keepdims=True))
    score_grad = (probs * (back_scores - row_delta) * score_scale).astype(jnp.bfloat16)
    sg_float = score_grad.astype(jnp.float32)
    grad_q = jnp.einsum('hqk,khd->qhd', sg_float, keys_rep).astype(jnp.bfloat16)
    grad_k_heads = jnp.einsum('hqk,qhd->khd', sg_float, q_float)
    grad_v_heads = jnp.einsum('hqk,qhd->khd', probs_bf.astype(jnp.float32), g_float)
    grad_k = grad_k_heads.reshape(tok_count, KV_HEADS, group_size, -1).sum(axis=2).astype(jnp.bfloat16)
    grad_v = grad_v_heads.reshape(tok_count, KV_HEADS, group_size, -1).sum(axis=2).astype(jnp.bfloat16)
    return (attended, grad_q, grad_k, grad_v)

def reference(layer_input, norm_gain, w_query, w_kv, lengths, out_grad):
    x_float = layer_input.astype(jnp.float32)
    inv_rms = lax.rsqrt(lax.optimization_barrier(jnp.mean(x_float * x_float, axis=1, keepdims=True)) + 1e-05)
    normed = (x_float * inv_rms * norm_gain[None, :]).astype(jnp.bfloat16)
    query_act = jnp.dot(normed, w_query, preferred_element_type=jnp.float32).astype(jnp.bfloat16)
    kv_act = jnp.dot(normed, w_kv, preferred_element_type=jnp.float32).astype(jnp.bfloat16)
    micro_count = lengths.shape[0]
    split_q = query_act.reshape(micro_count, TOK_DEV, HEADS, HD)
    split_k = kv_act[:, :KV_HEADS * HD].reshape(micro_count, TOK_DEV, KV_HEADS, HD)
    split_v = kv_act[:, KV_HEADS * HD:].reshape(micro_count, TOK_DEV, KV_HEADS, HD)
    split_g = out_grad.reshape(micro_count, TOK_DEV, HEADS, HD)
    results = lax.map(lambda packed: attend(*packed), (split_q, split_k, split_v, split_g, lengths))
    attended_all, grad_q, grad_k, grad_v = results
    total_rows = micro_count * TOK_DEV
    attn_out = attended_all.reshape(total_rows, HEADS * HD)
    grad_q = grad_q.reshape(total_rows, HEADS * HD)
    grad_kv_act = jnp.concatenate([grad_k.reshape(total_rows, KV_HEADS * HD), grad_v.reshape(total_rows, KV_HEADS * HD)], axis=1)
    grad_query = jnp.dot(normed.T, grad_q, preferred_element_type=jnp.float32)
    grad_kv = jnp.dot(normed.T, grad_kv_act, preferred_element_type=jnp.float32)
    return (attn_out, grad_query, grad_kv)
```

```python
import functools

import jax
import jax.numpy as jnp
from jax import lax
from jax.experimental import pallas as pl
from jax.experimental.pallas import tpu as pltpu
from jax.sharding import PartitionSpec as P

HEADS = 32
KV_HEADS = 4
HD = 128
RING = 8
BLK = 512
TOK = 512
HALF = BLK // 2
BF = jnp.bfloat16
F32 = jnp.float32
VMEM_LIMIT = 48 * 1024 * 1024


def ring_perm(step):
    return [(p, (p + 2 * step) % (2 * RING)) for p in range(2 * RING)]


CORE = [(p, p ^ 1) for p in range(2 * RING)]
DP = [(0, 1), (1, 0)]
KV_OUT_A = [(g, 2 * g) for g in range(4)] + [(4 + g, 2 * g + 1) for g in range(4)]
KV_OUT_B = [(g, 2 * g + 1) for g in range(4)] + [(4 + g, 2 * g) for g in range(4)]
KV_IN_A = [(d, s) for s, d in KV_OUT_A]
KV_IN_B = [(d, s) for s, d in KV_OUT_B]


def params():
    return pltpu.CompilerParams(vmem_limit_bytes=VMEM_LIMIT)


def norm_body(core_ref, x_ref, gain_ref, mine_ref, other_ref):
    core = core_ref[0]
    total = jnp.zeros((x_ref.shape[0], 1), F32)
    for j in range(2 * RING):
        part = x_ref[:, j * BLK : (j + 1) * BLK].astype(F32)
        total = total + jnp.sum(part * part, axis=1, keepdims=True)
    inv = lax.rsqrt(total / (2 * RING * BLK) + 1e-05)
    for ref, parity in ((mine_ref, core), (other_ref, 1 - core)):
        for i in range(RING):
            cols = pl.ds(pl.multiple_of((2 * i + parity) * BLK, BLK), BLK)
            part = x_ref[:, cols].astype(F32) * inv * gain_ref[:, cols]
            ref[i] = part.astype(BF)


def norm_split(x, gain, core):
    rows = 64
    out = jax.ShapeDtypeStruct((RING, TOK, BLK), BF)
    spec = pl.BlockSpec((RING, rows, BLK), lambda i, s: (0, i, 0))
    return pl.pallas_call(
        norm_body,
        grid_spec=pltpu.PrefetchScalarGridSpec(
            num_scalar_prefetch=1,
            grid=(TOK // rows,),
            in_specs=[
                pl.BlockSpec((rows, 2 * RING * BLK), lambda i, s: (i, 0)),
                pl.BlockSpec((1, 2 * RING * BLK), lambda i, s: (0, 0)),
            ],
            out_specs=[spec, spec],
        ),
        out_shape=[out, out],
        compiler_params=params(),
        cost_estimate=pl.CostEstimate(
            flops=6 * x.size, bytes_accessed=4 * x.size, transcendentals=TOK
        ),
        name="norm_split",
    )(core.reshape(1), x, gain.reshape(1, -1))


def fwd_body(count, halves, first, *refs):
    refs = refs[1:]
    own = refs[:count]
    oth = refs[count : 2 * count]
    w = refs[2 * count : 2 * count + (2 if halves else count)]
    rest = refs[2 * count + len(w) :]
    for xs, slot in ((own, 0), (oth, 1)):
        if halves:
            x = xs[0][0]
            out = jnp.dot(x[:, :HALF], w[0][...], preferred_element_type=F32)
            out = out + jnp.dot(x[:, HALF:], w[1][...], preferred_element_type=F32)
        else:
            out = jnp.dot(xs[0][0], w[0][...], preferred_element_type=F32)
            for k in range(1, count):
                out = out + jnp.dot(xs[k][0], w[k][...], preferred_element_type=F32)
        if first:
            rest[slot][...] = out
        else:
            rest[2 + slot][...] = rest[slot][...] + out


def fwd_step(mine, theirs, places, weights, accs, halves=False):
    rows = 256
    count = len(places)
    cols = weights[0].shape[1]
    first = accs is None

    def x_spec(k):
        return pl.BlockSpec((1, rows, BLK), lambda i, s: (s[k], i, 0))

    whole = [pl.BlockSpec(w.shape, lambda i, s: (0, 0)) for w in weights]
    acc_spec = pl.BlockSpec((rows, cols), lambda i, s: (i, 0))
    out = jax.ShapeDtypeStruct((TOK, cols), F32)
    return pl.pallas_call(
        functools.partial(fwd_body, count, halves, first),
        grid_spec=pltpu.PrefetchScalarGridSpec(
            num_scalar_prefetch=1,
            grid=(TOK // rows,),
            in_specs=[x_spec(k) for k in range(count)] * 2
            + whole
            + ([] if first else [acc_spec] * 2),
            out_specs=[acc_spec, acc_spec],
        ),
        out_shape=[out, out],
        compiler_params=params(),
        cost_estimate=pl.CostEstimate(
            flops=4 * TOK * BLK * cols * count,
            bytes_accessed=count * (4 * TOK * BLK + 2 * BLK * cols) + 16 * TOK * cols,
            transcendentals=0,
        ),
        name="fwd_step",
    )(
        jnp.stack(places).astype(jnp.int32),
        *([mine] * count),
        *([theirs] * count),
        *weights,
        *(() if first else accs),
    )


def attn_body(bounds_ref, q_ref, k_ref, v_ref, g_ref, o_ref, gq_ref, gk_ref, gv_ref):
    scale = HD ** (-0.5)
    rows = 256
    nt = (((1,), (1,)), ((), ()))

    @pl.when(pl.program_id(0) == 0)
    def _():
        gk_ref[...] = jnp.zeros_like(gk_ref)
        gv_ref[...] = jnp.zeros_like(gv_ref)

    for i in range(TOK // rows):
        keys = (i + 1) * rows
        here = slice(i * rows, (i + 1) * rows)
        q = q_ref[here, :]
        g = g_ref[here, :]
        k = k_ref[:keys, :]
        v = v_ref[:keys, :]
        row = lax.broadcasted_iota(jnp.int32, (rows, 1), 0) + i * rows
        col = lax.broadcasted_iota(jnp.int32, (1, keys), 1)
        start = jnp.zeros((rows, 1), jnp.int32)
        for d in range(3):
            start = jnp.where(row >= bounds_ref[d], bounds_ref[d], start)
        allowed = (col <= row) & (col >= start)
        s = lax.dot_general(q, k, nt, preferred_element_type=F32) * scale
        s = jnp.where(allowed, s, -1e30)
        e = jnp.exp(s - jnp.max(s, axis=1, keepdims=True))
        p = e / jnp.sum(e, axis=1, keepdims=True)
        pb = p.astype(BF)
        o_ref[here, :] = jnp.dot(pb, v, preferred_element_type=F32).astype(BF)
        b = lax.dot_general(g, v, nt, preferred_element_type=F32)
        delta = jnp.sum(p * b, axis=1, keepdims=True)
        sg = (p * (b - delta) * scale).astype(BF)
        gq = jnp.dot(sg, k, preferred_element_type=F32)
        gq_ref[:, here] = gq.T.astype(BF)
        gk_ref[:, :keys] += jnp.dot(q.T, sg, preferred_element_type=F32)
        gv_ref[:, :keys] += jnp.dot(g.T, pb, preferred_element_type=F32)


def attention(bounds, act, q_col, k, v, out_grad, g_col, heads):
    col = jax.ShapeDtypeStruct((TOK, heads * HD), BF)
    grad = jax.ShapeDtypeStruct((heads * HD, TOK), BF)
    kv_out = jax.ShapeDtypeStruct((HD, TOK), F32)
    whole = pl.BlockSpec((TOK, HD), lambda h, s: (0, 0))
    whole_t = pl.BlockSpec((HD, TOK), lambda h, s: (0, 0))
    return pl.pallas_call(
        attn_body,
        grid_spec=pltpu.PrefetchScalarGridSpec(
            num_scalar_prefetch=1,
            grid=(heads,),
            in_specs=[
                pl.BlockSpec((TOK, HD), lambda h, s: (0, q_col + h)),
                whole,
                whole,
                pl.BlockSpec((TOK, HD), lambda h, s: (0, g_col + h)),
            ],
            out_specs=[
                pl.BlockSpec((TOK, HD), lambda h, s: (0, h)),
                pl.BlockSpec((HD, TOK), lambda h, s: (h, 0)),
                whole_t,
                whole_t,
            ],
        ),
        out_shape=[col, grad, kv_out, kv_out],
        compiler_params=params(),
        cost_estimate=pl.CostEstimate(
            flops=24 * heads * TOK * TOK * HD,
            bytes_accessed=8 * heads * TOK * HD,
            transcendentals=heads * TOK * TOK,
        ),
        name="attention",
    )(bounds, act, k, v, out_grad)


def bwd_body(kind, *refs):
    refs = refs[1:]
    if kind == "first":
        own, oth, a_own, a_oth, f_out, b_out = refs
        for lanes, out in ((slice(0, HALF), f_out), (slice(HALF, BLK), b_out)):
            g = jnp.dot(a_own[...], own[0][:, lanes], preferred_element_type=F32)
            g = g + jnp.dot(a_oth[...], oth[0][:, lanes], preferred_element_type=F32)
            out[...] = g.astype(BF)
    elif kind == "last":
        own, oth, a_own, a_oth, f_in, b_in, out = refs
        g = jnp.dot(a_own[...], own[0], preferred_element_type=F32)
        g = g + jnp.dot(a_oth[...], oth[0], preferred_element_type=F32)
        out[...] = g + f_in[...].astype(F32) + b_in[...].astype(F32)
    else:
        own_f, oth_f, own_b, oth_b, a_own, a_oth, f_in, b_in, f_out, b_out = refs
        for own, oth, got, out, start in (
            (own_f, oth_f, f_in, f_out, 0),
            (own_b, oth_b, b_in, b_out, HALF),
        ):
            g = jnp.dot(a_own[...], own[0], preferred_element_type=F32)
            g = g + jnp.dot(a_oth[...], oth[0], preferred_element_type=F32)
            if kind == "second":
                lanes = slice(start, start + HALF)
                rest = slice(HALF - start, BLK - start)
                out[:, lanes] = (g[:, lanes] + got[...].astype(F32)).astype(BF)
                out[:, rest] = g[:, rest].astype(BF)
            else:
                out[...] = (g + got[...].astype(F32)).astype(BF)


def bwd_step(kind, mine, theirs, places, a_own, a_oth, got):
    cols = a_own.shape[0]
    rows = cols
    while rows > 256 or cols % rows:
        rows -= 128
    xs = []
    specs = []
    for k in range(len(places)):
        for x in (mine, theirs):
            xs.append(x)
            specs.append(pl.BlockSpec((1, TOK, BLK), lambda i, s, k=k: (s[k], 0, 0)))
    a_spec = pl.BlockSpec((rows, TOK), lambda i, s: (i, 0))

    def out_spec(width):
        return pl.BlockSpec((rows, width), lambda i, s: (i, 0))

    if kind == "last":
        outs = [jax.ShapeDtypeStruct((cols, BLK), F32)]
    else:
        width = HALF if kind == "first" else BLK
        outs = [jax.ShapeDtypeStruct((cols, width), BF)] * 2
    return pl.pallas_call(
        functools.partial(bwd_body, kind),
        grid_spec=pltpu.PrefetchScalarGridSpec(
            num_scalar_prefetch=1,
            grid=(cols // rows,),
            in_specs=specs + [a_spec, a_spec] + [out_spec(r.shape[1]) for r in got],
            out_specs=[out_spec(o.shape[1]) for o in outs],
        ),
        out_shape=outs,
        compiler_params=params(),
        cost_estimate=pl.CostEstimate(
            flops=4 * cols * TOK * BLK * len(places),
            bytes_accessed=4 * TOK * BLK * len(places) + 8 * cols * BLK,
            transcendentals=0,
        ),
        name="bwd_step",
    )(jnp.stack(places).astype(jnp.int32), *xs, a_own, a_oth, *got)


def gather_chain(w):
    f = b = w
    steps = []
    for _ in range(3):
        f = lax.ppermute(f, "pipe", ring_perm(1))
        b = lax.ppermute(b, "pipe", ring_perm(-1))
        steps.append((f, b))
    f = lax.ppermute(f[:HALF], "pipe", ring_perm(1))
    b = lax.ppermute(b[HALF:], "pipe", ring_perm(-1))
    steps.append((f, b))
    return steps


def local(layer_input, norm_gain, w_query, w_kv, lengths, out_grad):
    pipe = lax.axis_index("pipe")
    z, core = pipe // 2, pipe % 2
    odd = lax.axis_index("tensor") % 2
    dp = lax.axis_index("dp")
    bounds = jnp.cumsum(lengths[0])[:3].astype(jnp.int32)

    def at(offset):
        return (z + offset + RING) % RING

    mine, other = norm_split(layer_input, norm_gain, core)
    theirs = lax.ppermute(other, "pipe", CORE)

    def project(w):
        steps = gather_chain(w)
        accs = fwd_step(
            mine, theirs, [at(0), at(-1), at(1)], [w, *steps[0]], None
        )
        accs = fwd_step(mine, theirs, [at(-2), at(2)], steps[1], accs)
        accs = fwd_step(mine, theirs, [at(-3), at(3)], steps[2], accs)
        accs = fwd_step(mine, theirs, [at(4)], steps[3], accs, halves=True)
        return (accs[0] + lax.ppermute(accs[1], "pipe", CORE)).astype(BF)

    def weight_grad(a_own):
        a_oth = lax.ppermute(a_own, "pipe", CORE)
        f, b = bwd_step("first", mine, theirs, [at(4)], a_own, a_oth, [])
        for kind, s in (("second", 3), ("more", 2), ("more", 1)):
            f = lax.ppermute(f, "pipe", ring_perm(1))
            b = lax.ppermute(b, "pipe", ring_perm(-1))
            f, b = bwd_step(kind, mine, theirs, [at(s), at(-s)], a_own, a_oth, [f, b])
        f = lax.ppermute(f, "pipe", ring_perm(1))
        b = lax.ppermute(b, "pipe", ring_perm(-1))
        (g,) = bwd_step("last", mine, theirs, [at(0)], a_own, a_oth, [f, b])
        keep = lax.dynamic_slice_in_dim(g, dp * HALF, HALF, 1)
        give = lax.dynamic_slice_in_dim(g, (1 - dp) * HALF, HALF, 1).astype(BF)
        got = lax.ppermute(give, "dp", DP)
        return (keep + got.astype(F32)).T

    act_a = project(jnp.concatenate([w_kv, w_query[:, :256]], axis=1))
    act_b = project(w_query[:, 256:])

    kv = act_a[:, :HD]
    got_a = lax.ppermute(kv, "tensor", KV_OUT_A)
    got_b = lax.ppermute(kv, "tensor", KV_OUT_B)
    k = jnp.where(odd == 1, got_b, got_a)
    v = jnp.where(odd == 1, got_a, got_b)

    o_a, gq_a, gk_a, gv_a = attention(bounds, act_a, 1, k, v, out_grad, 0, 2)
    grad_a = weight_grad(gq_a)
    o_b, gq_b, gk_b, gv_b = attention(bounds, act_b, 0, k, v, out_grad, 2, 2)
    gk, gv = gk_a + gk_b, gv_a + gv_b
    kv_a = lax.ppermute(jnp.where(odd == 1, gv, gk), "tensor", KV_IN_A)
    kv_b = lax.ppermute(jnp.where(odd == 1, gk, gv), "tensor", KV_IN_B)
    gkv = (kv_a + kv_b).astype(BF)
    grad_b = weight_grad(jnp.concatenate([gq_b, gkv], axis=0))

    attn_out = jnp.concatenate([o_a, o_b], axis=1)
    grad_query = jnp.concatenate([grad_a, grad_b[:, :256]], axis=1)
    return attn_out, grad_query, grad_b[:, 256:]


def solution(mesh):
    placed = (
        P(("pipe", "dp"), None),
        P(),
        P("pipe", "tensor"),
        P("pipe", "tensor"),
        P(("pipe", "dp"), None),
        P(("pipe", "dp"), "tensor"),
    )
    return jax.shard_map(
        local,
        mesh=mesh,
        in_specs=placed,
        out_specs=(
            P(("pipe", "dp"), "tensor"),
            P(("pipe", "dp"), "tensor"),
            P(("pipe", "dp"), "tensor"),
        ),
        check_vma=False,
    )
```

```python
import functools

import jax
import jax.numpy as jnp
from jax import lax
from jax.experimental import pallas as pl
from jax.experimental.pallas import tpu as pltpu
from jax.sharding import PartitionSpec as P

HEADS = 32
KV_HEADS = 4
HD = 128
RING = 8
BLK = 512
TOK = 512
HALF = BLK // 2
WINDOWS = 4
BF = jnp.bfloat16
F32 = jnp.float32


def ring_perm(step):
    return [(p, (p + 2 * step) % (2 * RING)) for p in range(2 * RING)]


CORE = [(p, p ^ 1) for p in range(2 * RING)]
DP = [(0, 1), (1, 0)]
VMEM = pl.BlockSpec(memory_space=pltpu.VMEM)
SMEM = pl.BlockSpec(memory_space=pltpu.SMEM)
COST = pl.CostEstimate(flops=1, bytes_accessed=1, transcendentals=0)
KV_OUT_A = [(g, 2 * g) for g in range(4)] + [(4 + g, 2 * g + 1) for g in range(4)]
KV_OUT_B = [(g, 2 * g + 1) for g in range(4)] + [(4 + g, 2 * g) for g in range(4)]
PAIR = [(t, t ^ 1) for t in range(8)]
KV_HOME = [(2 * g, g) for g in range(4)] + [(2 * g + 1, 4 + g) for g in range(4)]


def params(mib=8):
    return pltpu.CompilerParams(vmem_limit_bytes=mib * 1024 * 1024)


def norm_body(core_ref, *refs):
    x_refs, (gain_ref, mine_ref, other_ref) = refs[:WINDOWS], refs[WINDOWS:]
    core = core_ref[0]
    rows, wide = x_refs[0].shape
    here = pl.ds(pl.multiple_of(pl.program_id(0) * rows, rows), rows)
    total = jnp.zeros((rows, HD), F32)
    for x_ref in x_refs:
        for j in range(wide // HD):
            part = x_ref[:, j * HD : (j + 1) * HD].astype(F32)
            total = total + part * part
    mean = jnp.sum(total, axis=1, keepdims=True) / (wide * WINDOWS)
    inv = lax.rsqrt(mean + 1e-05)
    for dst, parity in ((mine_ref, core), (other_ref, 1 - core)):
        for i in range(RING):
            first = 2 * BLK * i
            cols = pl.ds(pl.multiple_of(first % wide + parity * BLK, BLK), BLK)
            part = x_refs[first // wide][:, cols].astype(F32) * inv
            cols = pl.ds(pl.multiple_of(first + parity * BLK, BLK), BLK)
            part = part * gain_ref[:, cols]
            dst[i, here, :] = part.astype(BF)


def norm_split(x, gain, core):
    rows = 64
    out = jax.ShapeDtypeStruct((RING, TOK, BLK), BF)
    return pl.pallas_call(
        norm_body,
        grid_spec=pltpu.PrefetchScalarGridSpec(
            num_scalar_prefetch=1,
            grid=(TOK // rows,),
            in_specs=[
                pl.BlockSpec(
                    (rows, 2 * RING * BLK // WINDOWS), lambda i, s, k=k: (i, k)
                )
                for k in range(WINDOWS)
            ]
            + [pl.BlockSpec((1, 2 * RING * BLK), lambda i, s: (0, 0))],
            out_specs=[VMEM, VMEM],
        ),
        out_shape=[out, out],
        compiler_params=params(52),
        cost_estimate=COST,
        name="norm_split",
    )(core, *([x] * WINDOWS), gain)


def fwd_body(plan, first, place_ref, mine_ref, theirs_ref, *refs):
    weights, rest = refs[: len(plan)], refs[len(plan) :]
    rows = 256
    for slot, x_ref in enumerate((mine_ref, theirs_ref)):
        for i in range(TOK // rows):
            here = slice(i * rows, (i + 1) * rows)
            out = jnp.zeros((rows, weights[0].shape[1]), F32)
            if not first:
                out = rest[slot][here, :]
            for (at, start), w in zip(plan, weights, strict=True):
                x = x_ref[place_ref[at], here, start : start + w.shape[0]]
                out = out + jnp.dot(x, w[...], preferred_element_type=F32)
            rest[slot - 2][here, :] = out


def fwd_step(mine, theirs, places, plan, weights, accs):
    cols = weights[0].shape[1]
    first = accs is None
    accs = [] if first else accs
    out = jax.ShapeDtypeStruct((TOK, cols), F32)
    return pl.pallas_call(
        functools.partial(fwd_body, plan, first),
        in_specs=[SMEM] + [VMEM] * (2 + len(weights) + len(accs)),
        out_specs=[VMEM, VMEM],
        out_shape=[out, out],
        compiler_params=params(),
        cost_estimate=COST,
        name="fwd_step",
    )(places, mine, theirs, *weights, *accs)


def attn_body(bounds_ref, q_ref, k_ref, v_ref, g_ref, o_ref, gq_ref, gk_ref, gv_ref):
    scale = HD ** (-0.5)
    rows = 256
    nt = (((1,), (1,)), ((), ()))

    @pl.when(pl.program_id(0) == 0)
    def _():
        gk_ref[...] = jnp.zeros_like(gk_ref)
        gv_ref[...] = jnp.zeros_like(gv_ref)

    for i in range(TOK // rows):
        keys = (i + 1) * rows
        here = slice(i * rows, (i + 1) * rows)
        q = q_ref[here, :]
        g = g_ref[here, :]
        k = k_ref[:keys, :]
        v = v_ref[:keys, :]
        row = lax.broadcasted_iota(jnp.int32, (rows, 1), 0) + i * rows
        col = lax.broadcasted_iota(jnp.int32, (1, keys), 1)
        start = jnp.zeros((rows, 1), jnp.int32)
        for d in range(3):
            start = jnp.where(row >= bounds_ref[d], bounds_ref[d], start)
        allowed = (col <= row) & (col >= start)
        s = lax.dot_general(q, k, nt, preferred_element_type=F32) * scale
        s = jnp.where(allowed, s, -1e30)
        e = jnp.exp(s - jnp.max(s, axis=1, keepdims=True))
        p = e / jnp.sum(e, axis=1, keepdims=True)
        pb = p.astype(BF)
        o_ref[here, :] = jnp.dot(pb, v, preferred_element_type=F32).astype(BF)
        b = lax.dot_general(g, v, nt, preferred_element_type=F32)
        delta = jnp.sum(p * b, axis=1, keepdims=True)
        sg = (p * (b - delta) * scale).astype(BF)
        gq = jnp.dot(sg, k, preferred_element_type=F32)
        gq_ref[:, here] = gq.T.astype(BF)
        gk_ref[:, :keys] += jnp.dot(q.T, sg, preferred_element_type=F32)
        gv_ref[:, :keys] += jnp.dot(g.T, pb, preferred_element_type=F32)


def attention(bounds, q, k, v, out_grad, col, heads):
    out = jax.ShapeDtypeStruct((TOK, heads * HD), BF)
    grad = jax.ShapeDtypeStruct((heads * HD, TOK), BF)
    kv_out = jax.ShapeDtypeStruct((HD, TOK), F32)
    whole = pl.BlockSpec((TOK, HD), lambda h, s: (0, 0))
    whole_t = pl.BlockSpec((HD, TOK), lambda h, s: (0, 0))
    return pl.pallas_call(
        attn_body,
        grid_spec=pltpu.PrefetchScalarGridSpec(
            num_scalar_prefetch=1,
            grid=(heads,),
            in_specs=[
                pl.BlockSpec((TOK, HD), lambda h, s: (0, col + h)),
                whole,
                whole,
                pl.BlockSpec((TOK, HD), lambda h, s: (0, col + h)),
            ],
            out_specs=[
                pl.BlockSpec((TOK, HD), lambda h, s: (0, h)),
                pl.BlockSpec((HD, TOK), lambda h, s: (h, 0)),
                whole_t,
                whole_t,
            ],
        ),
        out_shape=[out, grad, kv_out, kv_out],
        compiler_params=params(12),
        cost_estimate=COST,
        name="attention",
    )(bounds, q, k, v, out_grad)


def grad_body(place_ref, mine_ref, theirs_ref, own_ref, oth_ref, out_ref):
    def block(i, _):
        at = place_ref[i]
        g = jnp.dot(own_ref[...], mine_ref[at], preferred_element_type=F32)
        g += jnp.dot(oth_ref[...], theirs_ref[at], preferred_element_type=F32)
        out_ref[i] = g.astype(out_ref.dtype)
        return 0

    lax.fori_loop(0, out_ref.shape[0], block, 0)


def grad_blocks(places, mine, theirs, a_own, a_oth, dtype):
    shape = (places.shape[0], a_own.shape[0], BLK)
    return pl.pallas_call(
        grad_body,
        in_specs=[SMEM] + [VMEM] * 4,
        out_specs=VMEM,
        out_shape=jax.ShapeDtypeStruct(shape, dtype),
        compiler_params=params(),
        cost_estimate=COST,
        name="grad_blocks",
    )(places, mine, theirs, a_own, a_oth)


def split_body(q_ref, kv_ref, a_ref, b_ref):
    for rows, out in ((slice(0, HALF), a_ref), (slice(HALF, BLK), b_ref)):
        out[:, :BLK] = q_ref[rows, :]
        out[:, BLK:] = kv_ref[rows, :]


def split_weights(w_query, w_kv):
    out = jax.ShapeDtypeStruct((HALF, BLK + HD), BF)
    return pl.pallas_call(
        split_body,
        out_shape=[out, out],
        compiler_params=params(),
        cost_estimate=COST,
        name="split_weights",
    )(w_query, w_kv)


def both_ways(f, b):
    f = lax.ppermute(f, "pipe", ring_perm(1))
    b = lax.ppermute(b, "pipe", ring_perm(-1))
    return lax.optimization_barrier((f, b))


def local(layer_input, norm_gain, w_query, w_kv, lengths, out_grad):
    pipe = lax.axis_index("pipe")
    z, core = pipe // 2, (pipe % 2).reshape(1)
    odd = lax.axis_index("tensor") % 2
    dp = lax.axis_index("dp")
    bounds = jnp.cumsum(lengths[0])[:3].astype(jnp.int32)

    def exchange(accs):
        return (accs[0] + lax.ppermute(accs[1], "pipe", CORE)).astype(BF)

    def grad_start(a_own, tied):
        a_oth = lax.ppermute(a_own, "pipe", CORE)
        first = grad_blocks(far, mine, theirs, a_own, a_oth, BF)[0]
        first, tied = lax.optimization_barrier((first, tied))
        return (first[:, :HALF], first[:, HALF:]), a_oth, tied

    def grad_second(got, a_own, a_oth):
        g = grad_blocks(near, mine, theirs, a_own, a_oth, F32)
        f = jnp.pad(got[0].astype(F32), ((0, 0), (0, HALF)))
        b = jnp.pad(got[1].astype(F32), ((0, 0), (HALF, 0)))
        return g, ((g[0] + f).astype(BF), (g[1] + b).astype(BF))

    def grad_ring(g, got):
        got = both_ways(*got)
        for s in range(1, 3):
            f, b = got[0].astype(F32), got[1].astype(F32)
            got = both_ways((g[2 * s] + f).astype(BF), (g[2 * s + 1] + b).astype(BF))
        g = g[6] + got[0].astype(F32) + got[1].astype(F32)
        keep = lax.dynamic_slice_in_dim(g, dp * HALF, HALF, 1)
        give = lax.dynamic_slice_in_dim(g, (1 - dp) * HALF, HALF, 1).astype(BF)
        got = lax.ppermute(give, "dp", DP)
        return (keep + got.astype(F32)).T

    def places(*offsets):
        return (z + jnp.array(offsets, jnp.int32)) % RING

    def tie(*values):
        return lax.optimization_barrier(values)

    far, near = places(4), places(3, 5, 2, 6, 1, 7, 0)
    around = places(0, 7, 1, 6, 2, 5, 3, 4)
    mine, other = norm_split(layer_input, norm_gain.reshape(1, -1), core)
    theirs = lax.ppermute(other, "pipe", CORE)

    a0, b0 = split_weights(w_query, w_kv)
    a1, b1 = both_ways(a0, a0), both_ways(b0, b0)
    a2, b2 = both_ways(*a1), both_ways(*b1)
    a3 = both_ways(*a2)
    plan = tuple((j, 0) for j in range(5))
    accs = fwd_step(mine, theirs, around, plan, [a0, *a1, *a2], None)
    b2, accs = tie(b2, accs)
    b3 = both_ways(*b2)
    plan = tuple((j, HALF) for j in range(5))
    accs = fwd_step(mine, theirs, around, plan, [b0, *b1, *b2], accs)
    a3, accs = tie(a3, accs)
    a4 = both_ways(a3[0][:HD], a3[1][HD:])
    b4 = both_ways(b3[0][:HD], b3[1][HD:])
    plan = ((5, 0), (6, 0), (5, HALF), (6, HALF))
    plan += tuple((7, start) for start in range(0, BLK, HD))
    accs = fwd_step(mine, theirs, around, plan, [*a3, *b3, *a4, *b4], accs)
    kv = exchange([p[:, BLK:] for p in accs])
    q = exchange([p[:, :BLK] for p in accs])

    got_a = lax.ppermute(kv, "tensor", KV_OUT_A)
    got_b = lax.ppermute(kv, "tensor", KV_OUT_B)
    k = jnp.where(odd == 1, got_b, got_a)
    v = jnp.where(odd == 1, got_a, got_b)
    o_a, gq_a, gk_a, gv_a = attention(bounds, q, k, v, out_grad, 0, 3)
    o_b, gq_b, gk_b, gv_b = attention(bounds, q, k, v, out_grad, 3, 1)
    gk, gv = gk_a + gk_b, gv_a + gv_b
    first_a, oth_a, (gk, gv) = grad_start(gq_a, (gk, gv))
    got = lax.ppermute(jnp.where(odd == 1, gk, gv), "tensor", PAIR)
    gkv = (jnp.where(odd == 1, gv, gk) + got).astype(BF)
    g_a, second_a = grad_second(both_ways(*first_a), gq_a, oth_a)
    gkv, second_a = tie(gkv, second_a)
    gkv = lax.ppermute(gkv, "tensor", KV_HOME)
    a_b = jnp.concatenate([gq_b, gkv], axis=0)
    first_b, oth_b, _ = grad_start(a_b, ())
    grad_a = grad_ring(g_a, second_a)
    grad_b = grad_ring(*grad_second(both_ways(*first_b), a_b, oth_b))

    attn_out = jnp.concatenate([o_a, o_b], axis=1)
    grad_query = jnp.concatenate([grad_a, grad_b[:, :HD]], axis=1)
    return attn_out, grad_query, grad_b[:, HD:]


def solution(mesh):
    placed = (
        P(("pipe", "dp"), None),
        P(),
        P("pipe", "tensor"),
        P("pipe", "tensor"),
        P(("pipe", "dp"), None),
        P(("pipe", "dp"), "tensor"),
    )
    return jax.shard_map(
        local,
        mesh=mesh,
        in_specs=placed,
        out_specs=(
            P(("pipe", "dp"), "tensor"),
            P(("pipe", "dp"), "tensor"),
            P(("pipe", "dp"), "tensor"),
        ),
        check_vma=False,
    )
```

```python
import functools

import jax
import jax.numpy as jnp
from jax import lax
from jax.experimental import pallas as pl
from jax.experimental.pallas import tpu as pltpu
from jax.sharding import PartitionSpec as P

HEADS = 32
KV_HEADS = 4
HD = 128
RING = 8
BLK = 512
TOK = 512
HALF = BLK // 2
EACH = 4
ORDER = (0, 7, 1, 6, 2, 5, 3, 4)
BF = jnp.bfloat16
F32 = jnp.float32


def ring_perm(step):
    return [(p, (p + 2 * step) % (2 * RING)) for p in range(2 * RING)]


CORE = [(p, p ^ 1) for p in range(2 * RING)]
DP = [(0, 1), (1, 0)]
VMEM = pl.BlockSpec(memory_space=pltpu.VMEM)
SMEM = pl.BlockSpec(memory_space=pltpu.SMEM)
COST = pl.CostEstimate(flops=1, bytes_accessed=1, transcendentals=0)
KV_OUT_A = [(g, 2 * g) for g in range(4)] + [(4 + g, 2 * g + 1) for g in range(4)]
KV_OUT_B = [(g, 2 * g + 1) for g in range(4)] + [(4 + g, 2 * g) for g in range(4)]
PAIR = [(t, t ^ 1) for t in range(8)]
KV_HOME = [(2 * g, g) for g in range(4)] + [(2 * g + 1, 4 + g) for g in range(4)]
KV_ACROSS = [(8 * p + t, 8 * (p ^ 1) + home) for p in range(16) for t, home in KV_HOME]


def params(mib=8):
    return pltpu.CompilerParams(vmem_limit_bytes=mib * 1024 * 1024)


def norm_body(place_ref, core_ref, x_ref, gain_ref, mine_ref, *other_refs):
    core = core_ref[0]
    rows = 32
    for start in range(0, x_ref.shape[0], rows):
        here = slice(start, start + rows)
        total = jnp.zeros((rows, HD), F32)
        for j in range(x_ref.shape[1] // HD):
            part = x_ref[here, j * HD : (j + 1) * HD].astype(F32)
            total = total + part * part
        mean = jnp.sum(total, axis=1, keepdims=True) / x_ref.shape[1]
        inv = lax.rsqrt(mean + 1e-05)
        for i in range(RING):
            for parity in (core, 1 - core):
                at = (2 * place_ref[i] + parity) * BLK
                cols = pl.ds(pl.multiple_of(at, BLK), BLK)
                part = x_ref[here, cols].astype(F32) * inv * gain_ref[:, cols]
                if parity is core:
                    mine_ref[i, here, :] = part.astype(BF)
                else:
                    other_refs[i // EACH][i % EACH, here, :] = part.astype(BF)


def norm_split(x, gain, places, core):
    rows = 128
    blocks = [RING] + [EACH] * (RING // EACH)
    return pl.pallas_call(
        norm_body,
        grid_spec=pltpu.PrefetchScalarGridSpec(
            num_scalar_prefetch=2,
            grid=(TOK // rows,),
            in_specs=[
                pl.BlockSpec((rows, 2 * RING * BLK), lambda i, s, t: (i, 0)),
                pl.BlockSpec((1, 2 * RING * BLK), lambda i, s, t: (0, 0)),
            ],
            out_specs=[pl.BlockSpec((n, rows, BLK), lambda i, s, t: (0, i, 0)) for n in blocks],
        ),
        out_shape=[jax.ShapeDtypeStruct((n, TOK, BLK), BF) for n in blocks],
        compiler_params=params(52),
        cost_estimate=COST,
        name="norm_split",
    )(places, core, x, gain)


def fwd_body(count, parts, first, *refs):
    own, oth, weights, rest = (
        refs[:count],
        refs[count : 2 * count],
        refs[2 * count : 3 * count],
        refs[3 * count :],
    )
    for k, (start, wide) in enumerate(parts):
        for slot, xs in ((2 * k, own), (2 * k + 1, oth)):
            out_ref = rest[slot - 2 * len(parts)]
            out = jnp.zeros(out_ref.shape, F32) if first else rest[slot][...]
            for x, w in zip(xs, weights, strict=True):
                w = w[:, start : start + wide]
                out = out + jnp.dot(x[0], w, preferred_element_type=F32)
            out_ref[...] = out


def fwd_step(mine, theirs, plan, weights, parts, accs=()):
    rows = 256
    def x_specs(each):
        return [
            pl.BlockSpec(
                (1, rows, w.shape[0]), lambda i, at=at, half=half: (at % each, i, half)
            )
            for (at, half), w in zip(plan, weights, strict=True)
        ]

    w_specs = [pl.BlockSpec(w.shape, lambda i: (0, 0)) for w in weights]
    acc_specs = [pl.BlockSpec((rows, wide), lambda i: (i, 0)) for _, wide in parts for _ in "ab"]
    return pl.pallas_call(
        functools.partial(fwd_body, len(weights), parts, not accs),
        grid=(TOK // rows,),
        in_specs=x_specs(RING) + x_specs(EACH) + w_specs + acc_specs[: len(accs)],
        out_specs=acc_specs,
        out_shape=[
            jax.ShapeDtypeStruct((TOK, wide), F32) for _, wide in parts for _ in "ab"
        ],
        compiler_params=params(20),
        cost_estimate=COST,
        name="fwd_step",
    )(
        *([mine] * len(plan)),
        *[theirs[at // EACH] for at, _ in plan],
        *weights,
        *accs,
    )


def attn_body(bounds_ref, q_ref, k_ref, v_ref, g_ref, o_ref, gq_ref, gk_ref, gv_ref):
    scale = HD ** (-0.5)
    rows = 256
    nt = (((1,), (1,)), ((), ()))

    @pl.when(pl.program_id(0) == 0)
    def _():
        gk_ref[...] = jnp.zeros_like(gk_ref)
        gv_ref[...] = jnp.zeros_like(gv_ref)

    for i in range(TOK // rows):
        keys = (i + 1) * rows
        here = slice(i * rows, (i + 1) * rows)
        q = q_ref[here, :]
        g = g_ref[here, :]
        k = k_ref[:keys, :]
        v = v_ref[:keys, :]
        row = lax.broadcasted_iota(jnp.int32, (rows, 1), 0) + i * rows
        col = lax.broadcasted_iota(jnp.int32, (1, keys), 1)
        start = jnp.zeros((rows, 1), jnp.int32)
        for d in range(3):
            start = jnp.where(row >= bounds_ref[d], bounds_ref[d], start)
        allowed = (col <= row) & (col >= start)
        s = lax.dot_general(q, k, nt, preferred_element_type=F32) * scale
        s = jnp.where(allowed, s, -1e30)
        e = jnp.exp(s - jnp.max(s, axis=1, keepdims=True))
        p = e / jnp.sum(e, axis=1, keepdims=True)
        pb = p.astype(BF)
        o_ref[here, :] = jnp.dot(pb, v, preferred_element_type=F32).astype(BF)
        b = lax.dot_general(g, v, nt, preferred_element_type=F32)
        delta = jnp.sum(p * b, axis=1, keepdims=True)
        sg = (p * (b - delta) * scale).astype(BF)
        gq = jnp.dot(sg, k, preferred_element_type=F32)
        gq_ref[:, here] = gq.T.astype(BF)
        gk_ref[:, :keys] += jnp.dot(q.T, sg, preferred_element_type=F32)
        gv_ref[:, :keys] += jnp.dot(g.T, pb, preferred_element_type=F32)


def attention(bounds, q, k, v, out_grad):
    heads = q.shape[1] // HD
    out = jax.ShapeDtypeStruct((TOK, heads * HD), BF)
    grad = jax.ShapeDtypeStruct((heads * HD, TOK), BF)
    kv_out = jax.ShapeDtypeStruct((HD, TOK), F32)
    whole = pl.BlockSpec((TOK, HD), lambda h, s: (0, 0))
    whole_t = pl.BlockSpec((HD, TOK), lambda h, s: (0, 0))
    return pl.pallas_call(
        attn_body,
        grid_spec=pltpu.PrefetchScalarGridSpec(
            num_scalar_prefetch=1,
            grid=(heads,),
            in_specs=[
                pl.BlockSpec((TOK, HD), lambda h, s: (0, h)),
                whole,
                whole,
                pl.BlockSpec((TOK, HD), lambda h, s: (0, h)),
            ],
            out_specs=[
                pl.BlockSpec((TOK, HD), lambda h, s: (0, h)),
                pl.BlockSpec((HD, TOK), lambda h, s: (h, 0)),
                whole_t,
                whole_t,
            ],
        ),
        out_shape=[out, grad, kv_out, kv_out],
        compiler_params=params(12),
        cost_estimate=COST,
        name="attention",
    )(bounds, q, k, v, out_grad)


def grad_body(kind, *refs):
    count = 2 if kind in ("second", "more") else 1
    xs, (own_ref, oth_ref), rest = refs[: 2 * count], refs[2 * count :][:2], refs[2 * count + 2 :]
    for i in range(count):
        g = jnp.dot(own_ref[...], xs[2 * i][0], preferred_element_type=F32)
        g += jnp.dot(oth_ref[...], xs[2 * i + 1][0], preferred_element_type=F32)
        if kind == "first":
            rest[0][...] = g[:, :HALF].astype(BF)
            rest[1][...] = g[:, HALF:].astype(BF)
        elif kind == "second":
            got, out = rest[i], rest[2 + i]
            hit = slice(i * HALF, (i + 1) * HALF)
            miss = slice((1 - i) * HALF, (2 - i) * HALF)
            out[:, hit] = (g[:, hit] + got[...].astype(F32)).astype(BF)
            out[:, miss] = g[:, miss].astype(BF)
        elif kind == "more":
            rest[2 + i][...] = (g + rest[i][...].astype(F32)).astype(BF)
        else:
            g = g + rest[0][...].astype(F32) + rest[1][...].astype(F32)
            low = rest[2][0] == 0
            rest[3][...] = jnp.where(low, g[:, :HALF], g[:, HALF:])
            rest[4][...] = jnp.where(low, g[:, HALF:], g[:, :HALF]).astype(BF)


def grad_step(kind, mine, theirs, blocks, a_own, a_oth, got=(), side=()):
    cols = a_own.shape[0]
    rows = cols // 2
    xs, x_specs = [], []
    for at in blocks:
        for x, j in ((mine, at), (theirs[at // EACH], at % EACH)):
            xs.append(x)
            x_specs.append(pl.BlockSpec((1, TOK, BLK), lambda i, j=j: (j, 0, 0)))
    a_spec = pl.BlockSpec((rows, TOK), lambda i: (i, 0))
    if kind == "last":
        outs = [jax.ShapeDtypeStruct((cols, HALF), dtype) for dtype in (F32, BF)]
    else:
        wide = HALF if kind == "first" else BLK
        outs = [jax.ShapeDtypeStruct((cols, wide), BF)] * 2

    def row_spec(x):
        return pl.BlockSpec((rows, x.shape[1]), lambda i: (i, 0))

    return pl.pallas_call(
        functools.partial(grad_body, kind),
        grid=(cols // rows,),
        in_specs=x_specs
        + [a_spec, a_spec]
        + [row_spec(x) for x in got]
        + [SMEM for _ in side],
        out_specs=[row_spec(x) for x in outs],
        out_shape=outs,
        compiler_params=params(16),
        cost_estimate=COST,
        name="grad_step",
    )(*xs, a_own, a_oth, *got, *side)


def join_body(a_ref, a_got_ref, b_ref, b_got_ref, q_ref, kv_ref):
    a = (a_ref[...] + a_got_ref[...].astype(F32)).T
    b = (b_ref[...] + b_got_ref[...].astype(F32)).T
    both = jnp.concatenate([a, b], axis=1)
    q_ref[...] = both[:, :BLK]
    kv_ref[...] = both[:, BLK:]


def join(*sums):
    return pl.pallas_call(
        join_body,
        out_shape=[
            jax.ShapeDtypeStruct((HALF, BLK), F32),
            jax.ShapeDtypeStruct((HALF, HD), F32),
        ],
        compiler_params=params(16),
        cost_estimate=COST,
        name="join",
    )(*sums)


def split_body(q_ref, kv_ref, a_ref, b_ref):
    for rows, out in ((slice(0, HALF), a_ref), (slice(HALF, BLK), b_ref)):
        out[:, :BLK] = q_ref[rows, :]
        out[:, BLK:] = kv_ref[rows, :]


def split_weights(w_query, w_kv):
    out = jax.ShapeDtypeStruct((HALF, BLK + HD), BF)
    return pl.pallas_call(
        split_body,
        out_shape=[out, out],
        compiler_params=params(),
        cost_estimate=COST,
        name="split_weights",
    )(w_query, w_kv)


def both_ways(f, b):
    f = lax.ppermute(f, "pipe", ring_perm(1))
    b = lax.ppermute(b, "pipe", ring_perm(-1))
    return lax.optimization_barrier((f, b))


def local(layer_input, norm_gain, w_query, w_kv, lengths, out_grad):
    pipe = lax.axis_index("pipe")
    z, core = pipe // 2, (pipe % 2).reshape(1)
    odd = lax.axis_index("tensor") % 2
    dp = lax.axis_index("dp")
    bounds = jnp.cumsum(lengths[0])[:3].astype(jnp.int32)

    def exchange(accs):
        return (accs[0] + lax.ppermute(accs[1], "pipe", CORE)).astype(BF)

    def grad(kind, offsets, own_oth, got=(), side=()):
        blocks = [ORDER.index(offset) for offset in offsets]
        return grad_step(kind, mine, theirs, blocks, *own_oth, got, side)

    def finish(own_oth, got):
        keep, give = grad("last", (0,), own_oth, got, (dp.reshape(1),))
        return keep, lax.ppermute(give, "dp", DP)

    def tie(*values):
        return lax.optimization_barrier(values)

    places = (z + jnp.array(ORDER, jnp.int32)) % RING
    a0, b0 = split_weights(w_query, w_kv)
    a1, b1 = both_ways(a0, a0), both_ways(b0, b0)
    mine, *other = norm_split(layer_input, norm_gain.reshape(1, -1), places, core)
    theirs = [lax.ppermute(x, "pipe", CORE) for x in other]
    a2, b2 = both_ways(*a1), both_ways(*b1)
    a3 = both_ways(*a2)
    parts = ((0, BLK), (BLK, HD))
    plan = tuple((j, 0) for j in range(5))
    accs = fwd_step(mine, theirs, plan, [a0, *a1, *a2], parts)
    b2, accs = tie(b2, accs)
    b3 = both_ways(*b2)
    plan = tuple((j, 1) for j in range(5))
    accs = fwd_step(mine, theirs, plan, [b0, *b1, *b2], parts, accs)
    a3, accs = tie(a3, accs)
    a4 = both_ways(a3[0][:HD], a3[1][HD:])
    b4 = both_ways(b3[0][:HD], b3[1][HD:])
    plan = ((5, 0), (6, 0), (5, 1), (6, 1))
    plan += tuple((7, quarter) for quarter in range(4))
    accs = fwd_step(mine, theirs, plan, [*a3, *b3, *a4, *b4], parts, accs)
    q, kv = exchange(accs[:2]), exchange(accs[2:])

    got_a = lax.ppermute(kv, "tensor", KV_OUT_A)
    got_b = lax.ppermute(kv, "tensor", KV_OUT_B)
    k = jnp.where(odd == 1, got_b, got_a)
    v = jnp.where(odd == 1, got_a, got_b)
    attn_out, gq, gk, gv = attention(bounds, q, k, v, out_grad)
    oth_q = lax.ppermute(gq, "pipe", CORE)
    split = 320
    act_a = gq[:split], oth_q[:split]
    step_a = grad("first", (4,), act_a)
    gk, gv, step_a = tie(gk, gv, step_a)
    got = lax.ppermute(jnp.where(odd == 1, gk, gv), "tensor", PAIR)
    gkv = (jnp.where(odd == 1, gv, gk) + got).astype(BF)
    step_a = both_ways(*step_a)
    gkv, step_a = tie(gkv, step_a)
    step_a = grad("second", (3, 5), act_a, step_a)
    step_a = both_ways(*step_a)
    own_kv = lax.ppermute(gkv, "tensor", KV_HOME)
    oth_kv = lax.ppermute(gkv, ("pipe", "tensor"), KV_ACROSS)
    act_b = (
        jnp.concatenate([gq[split:], own_kv], axis=0),
        jnp.concatenate([oth_q[split:], oth_kv], axis=0),
    )
    step_b = both_ways(*grad("first", (4,), act_b))
    step_a = both_ways(*grad("more", (2, 6), act_a, step_a))
    step_b = both_ways(*grad("second", (3, 5), act_b, step_b))
    step_a = both_ways(*grad("more", (1, 7), act_a, step_a))
    step_b = both_ways(*grad("more", (2, 6), act_b, step_b))
    step_b = both_ways(*grad("more", (1, 7), act_b, step_b))
    sums_a, sums_b = finish(act_a, step_a), finish(act_b, step_b)
    return attn_out, *join(*sums_a, *sums_b)


def solution(mesh):
    placed = (
        P(("pipe", "dp"), None),
        P(),
        P("pipe", "tensor"),
        P("pipe", "tensor"),
        P(("pipe", "dp"), None),
        P(("pipe", "dp"), "tensor"),
    )
    return jax.shard_map(
        local,
        mesh=mesh,
        in_specs=placed,
        out_specs=(
            P(("pipe", "dp"), "tensor"),
            P(("pipe", "dp"), "tensor"),
            P(("pipe", "dp"), "tensor"),
        ),
        check_vma=False,
    )
```

```python
import functools

import jax
import jax.numpy as jnp
from jax import lax
from jax.experimental import pallas as pl
from jax.experimental.pallas import tpu as pltpu
from jax.sharding import PartitionSpec as P

HEADS = 32
KV_HEADS = 4
HD = 128
RING = 8
BLK = 512
TOK = 512
HALF = BLK // 2
EACH = 4
ORDER = (0, 7, 1, 6, 2, 5, 3, 4)
BF = jnp.bfloat16
F32 = jnp.float32


def ring_perm(step):
    return [(p, (p + 2 * step) % (2 * RING)) for p in range(2 * RING)]


CORE = [(p, p ^ 1) for p in range(2 * RING)]
DP = [(0, 1), (1, 0)]
VMEM = pl.BlockSpec(memory_space=pltpu.VMEM)
SMEM = pl.BlockSpec(memory_space=pltpu.SMEM)
COST = pl.CostEstimate(flops=1, bytes_accessed=1, transcendentals=0)
KV_OUT_A = [(g, 2 * g) for g in range(4)] + [(4 + g, 2 * g + 1) for g in range(4)]
KV_OUT_B = [(g, 2 * g + 1) for g in range(4)] + [(4 + g, 2 * g) for g in range(4)]
PAIR = [(t, t ^ 1) for t in range(8)]
KV_HOME = [(2 * g, g) for g in range(4)] + [(2 * g + 1, 4 + g) for g in range(4)]
KV_ACROSS = [(8 * p + t, 8 * (p ^ 1) + home) for p in range(16) for t, home in KV_HOME]


def params(mib=8):
    return pltpu.CompilerParams(vmem_limit_bytes=mib * 1024 * 1024)


def norm_body(place_ref, core_ref, x_ref, gain_ref, mine_ref, *other_refs):
    core = core_ref[0]
    rows = 32
    for start in range(0, x_ref.shape[0], rows):
        here = slice(start, start + rows)
        total = jnp.zeros((rows, HD), F32)
        for j in range(x_ref.shape[1] // HD):
            part = x_ref[here, j * HD : (j + 1) * HD].astype(F32)
            total = total + part * part
        mean = jnp.sum(total, axis=1, keepdims=True) / x_ref.shape[1]
        inv = lax.rsqrt(mean + 1e-05)
        for i in range(RING):
            for parity in (core, 1 - core):
                at = (2 * place_ref[i] + parity) * BLK
                cols = pl.ds(pl.multiple_of(at, BLK), BLK)
                part = x_ref[here, cols].astype(F32) * inv * gain_ref[:, cols]
                if parity is core:
                    mine_ref[i, here, :] = part.astype(BF)
                else:
                    other_refs[i // EACH][i % EACH, here, :] = part.astype(BF)


def norm_split(x, gain, places, core):
    rows = 128
    blocks = [RING] + [EACH] * (RING // EACH)
    return pl.pallas_call(
        norm_body,
        grid_spec=pltpu.PrefetchScalarGridSpec(
            num_scalar_prefetch=2,
            grid=(TOK // rows,),
            in_specs=[
                pl.BlockSpec((rows, 2 * RING * BLK), lambda i, s, t: (i, 0)),
                pl.BlockSpec((1, 2 * RING * BLK), lambda i, s, t: (0, 0)),
            ],
            out_specs=[pl.BlockSpec((n, rows, BLK), lambda i, s, t: (0, i, 0)) for n in blocks],
        ),
        out_shape=[jax.ShapeDtypeStruct((n, TOK, BLK), BF) for n in blocks],
        compiler_params=params(42),
        cost_estimate=COST,
        name="norm_split",
    )(places, core, x, gain)


def fwd_body(groups, parts, first, *refs):
    count = len(groups)
    pieces = sum(n for _, n in groups)
    own, oth, weights, rest = (
        refs[:count],
        refs[count : 2 * count],
        refs[2 * count : 2 * count + pieces],
        refs[2 * count + pieces :],
    )
    blocks = []
    for _, n in groups:
        rows = [w[...] for w in weights[:n]]
        blocks.append(jnp.concatenate(rows, axis=0) if n > 1 else rows[0])
        weights = weights[n:]
    for k, (start, wide) in enumerate(parts):
        for slot, xs in ((2 * k, own), (2 * k + 1, oth)):
            out_ref = rest[slot - 2 * len(parts)]
            out = jnp.zeros(out_ref.shape, F32) if first else rest[slot][...]
            for x, w in zip(xs, blocks, strict=True):
                w = w[:, start : start + wide]
                out = out + jnp.dot(x[0], w, preferred_element_type=F32)
            out_ref[...] = out


def fwd_step(mine, theirs, groups, weights, parts, accs=()):
    rows = 256

    def x_specs(each):
        return [
            pl.BlockSpec((1, rows, BLK), lambda i, at=at: (at % each, i, 0))
            for at, _ in groups
        ]

    w_specs = [pl.BlockSpec(w.shape, lambda i: (0, 0)) for w in weights]
    acc_specs = [
        pl.BlockSpec((rows, wide), lambda i: (i, 0)) for _, wide in parts for _ in "ab"
    ]
    return pl.pallas_call(
        functools.partial(fwd_body, groups, parts, not accs),
        grid=(TOK // rows,),
        in_specs=x_specs(RING) + x_specs(EACH) + w_specs + acc_specs[: len(accs)],
        out_specs=acc_specs,
        out_shape=[
            jax.ShapeDtypeStruct((TOK, wide), F32) for _, wide in parts for _ in "ab"
        ],
        compiler_params=params(20),
        cost_estimate=COST,
        name="fwd_step",
    )(
        *([mine] * len(groups)),
        *[theirs[at // EACH] for at, _ in groups],
        *weights,
        *accs,
    )


def attn_body(
    bounds_ref, q_ref, k_ref, v_ref, g_ref, o_ref, gq_ref, gk_ref, gv_ref, bias_ref
):
    scale = HD ** (-0.5)
    rows = 256
    nt = (((1,), (1,)), ((), ()))

    @pl.when(pl.program_id(0) == 0)
    def _():
        gk_ref[...] = jnp.zeros_like(gk_ref)
        gv_ref[...] = jnp.zeros_like(gv_ref)
        row = lax.broadcasted_iota(jnp.int32, (TOK, 1), 0)
        col = lax.broadcasted_iota(jnp.int32, (1, TOK), 1)
        start = jnp.zeros((TOK, 1), jnp.int32)
        for d in range(3):
            start = jnp.where(row >= bounds_ref[d], bounds_ref[d], start)
        bias_ref[...] = jnp.where((col <= row) & (col >= start), 0.0, -1e30)

    for i in range(TOK // rows):
        keys = (i + 1) * rows
        here = slice(i * rows, (i + 1) * rows)
        q = q_ref[here, :]
        g = g_ref[here, :]
        k = k_ref[:keys, :]
        v = v_ref[:keys, :]
        s = lax.dot_general(q, k, nt, preferred_element_type=F32) * scale
        s = s + bias_ref[here, :keys]
        e = jnp.exp(s - jnp.max(s, axis=1, keepdims=True))
        p = e * (1.0 / jnp.sum(e, axis=1, keepdims=True))
        pb = p.astype(BF)
        o_ref[here, :] = jnp.dot(pb, v, preferred_element_type=F32).astype(BF)
        b = lax.dot_general(g, v, nt, preferred_element_type=F32)
        delta = jnp.sum(p * b, axis=1, keepdims=True)
        sg = (p * (b - delta) * scale).astype(BF)
        gq = jnp.dot(sg, k, preferred_element_type=F32)
        gq_ref[:, here] = gq.T.astype(BF)
        gk_ref[:, :keys] += jnp.dot(q.T, sg, preferred_element_type=F32)
        gv_ref[:, :keys] += jnp.dot(g.T, pb, preferred_element_type=F32)


def attention(bounds, q, k, v, out_grad):
    heads = out_grad.shape[1] // HD
    out = jax.ShapeDtypeStruct((TOK, heads * HD), BF)
    grad = jax.ShapeDtypeStruct((heads * HD, TOK), BF)
    kv_out = jax.ShapeDtypeStruct((HD, TOK), F32)
    whole = pl.BlockSpec((TOK, HD), lambda h, s: (0, 0))
    whole_t = pl.BlockSpec((HD, TOK), lambda h, s: (0, 0))
    return pl.pallas_call(
        attn_body,
        grid_spec=pltpu.PrefetchScalarGridSpec(
            num_scalar_prefetch=1,
            grid=(heads,),
            in_specs=[
                pl.BlockSpec((TOK, HD), lambda h, s: (0, h)),
                whole,
                whole,
                pl.BlockSpec((TOK, HD), lambda h, s: (0, h)),
            ],
            out_specs=[
                pl.BlockSpec((TOK, HD), lambda h, s: (0, h)),
                pl.BlockSpec((HD, TOK), lambda h, s: (h, 0)),
                whole_t,
                whole_t,
            ],
            scratch_shapes=[pltpu.VMEM((TOK, TOK), F32)],
        ),
        out_shape=[out, grad, kv_out, kv_out],
        compiler_params=params(12),
        cost_estimate=COST,
        name="attention",
    )(bounds, q, k, v, out_grad)


def grad_body(kind, *refs):
    count = 2 if kind in ("second", "more") else 1
    xs, (own_ref, oth_ref), rest = refs[: 2 * count], refs[2 * count :][:2], refs[2 * count + 2 :]
    for i in range(count):
        g = jnp.dot(own_ref[...], xs[2 * i][0], preferred_element_type=F32)
        g += jnp.dot(oth_ref[...], xs[2 * i + 1][0], preferred_element_type=F32)
        if kind == "first":
            rest[0][...] = g[:, :HALF].astype(BF)
            rest[1][...] = g[:, HALF:].astype(BF)
        elif kind == "second":
            got, out = rest[i], rest[2 + i]
            hit = slice(i * HALF, (i + 1) * HALF)
            miss = slice((1 - i) * HALF, (2 - i) * HALF)
            out[:, hit] = (g[:, hit] + got[...].astype(F32)).astype(BF)
            out[:, miss] = g[:, miss].astype(BF)
        elif kind == "more":
            rest[2 + i][...] = (g + rest[i][...].astype(F32)).astype(BF)
        else:
            g = g + rest[0][...].astype(F32) + rest[1][...].astype(F32)
            low = rest[2][0] == 0
            rest[3][...] = jnp.where(low, g[:, :HALF], g[:, HALF:])
            rest[4][...] = jnp.where(low, g[:, HALF:], g[:, :HALF]).astype(BF)


def grad_step(kind, mine, theirs, blocks, a_own, a_oth, got=(), side=()):
    cols = a_own.shape[0]
    rows = cols // 2
    xs, x_specs = [], []
    for at in blocks:
        for x, j in ((mine, at), (theirs[at // EACH], at % EACH)):
            xs.append(x)
            x_specs.append(pl.BlockSpec((1, TOK, BLK), lambda i, j=j: (j, 0, 0)))
    a_spec = pl.BlockSpec((rows, TOK), lambda i: (i, 0))
    if kind == "last":
        outs = [jax.ShapeDtypeStruct((cols, HALF), dtype) for dtype in (F32, BF)]
    else:
        wide = HALF if kind == "first" else BLK
        outs = [jax.ShapeDtypeStruct((cols, wide), BF)] * 2

    def row_spec(x):
        return pl.BlockSpec((rows, x.shape[1]), lambda i: (i, 0))

    return pl.pallas_call(
        functools.partial(grad_body, kind),
        grid=(cols // rows,),
        in_specs=x_specs
        + [a_spec, a_spec]
        + [row_spec(x) for x in got]
        + [SMEM for _ in side],
        out_specs=[row_spec(x) for x in outs],
        out_shape=outs,
        compiler_params=params(16),
        cost_estimate=COST,
        name="grad_step",
    )(*xs, a_own, a_oth, *got, *side)


def join_body(a_ref, a_got_ref, b_ref, b_got_ref, q_ref, kv_ref):
    a = (a_ref[...] + a_got_ref[...].astype(F32)).T
    b = (b_ref[...] + b_got_ref[...].astype(F32)).T
    both = jnp.concatenate([a, b], axis=1)
    q_ref[...] = both[:, :BLK]
    kv_ref[...] = both[:, BLK:]


def join(*sums):
    return pl.pallas_call(
        join_body,
        out_shape=[
            jax.ShapeDtypeStruct((HALF, BLK), F32),
            jax.ShapeDtypeStruct((HALF, HD), F32),
        ],
        compiler_params=params(16),
        cost_estimate=COST,
        name="join",
    )(*sums)


def split_body(q_ref, kv_ref, a_ref, b_ref):
    for rows, out in ((slice(0, HALF), a_ref), (slice(HALF, BLK), b_ref)):
        out[:, :BLK] = q_ref[rows, :]
        out[:, BLK:] = kv_ref[rows, :]


def split_weights(w_query, w_kv):
    out = jax.ShapeDtypeStruct((HALF, BLK + HD), BF)
    return pl.pallas_call(
        split_body,
        out_shape=[out, out],
        compiler_params=params(),
        cost_estimate=COST,
        name="split_weights",
    )(w_query, w_kv)


def both_ways(f, b):
    f = lax.ppermute(f, "pipe", ring_perm(1))
    b = lax.ppermute(b, "pipe", ring_perm(-1))
    return lax.optimization_barrier((f, b))


def local(layer_input, norm_gain, w_query, w_kv, lengths, out_grad):
    pipe = lax.axis_index("pipe")
    z, core = pipe // 2, (pipe % 2).reshape(1)
    odd = lax.axis_index("tensor") % 2
    dp = lax.axis_index("dp")
    bounds = jnp.cumsum(lengths[0])[:3].astype(jnp.int32)

    def exchange(accs):
        return (accs[0] + lax.ppermute(accs[1], "pipe", CORE)).astype(BF)

    def grad(kind, offsets, own_oth, got=(), side=()):
        blocks = [ORDER.index(offset) for offset in offsets]
        return grad_step(kind, mine, theirs, blocks, *own_oth, got, side)

    def finish(own_oth, got):
        keep, give = grad("last", (0,), own_oth, got, (dp.reshape(1),))
        return keep, lax.ppermute(give, "dp", DP)

    def tie(*values):
        return lax.optimization_barrier(values)

    places = (z + jnp.array(ORDER, jnp.int32)) % RING
    a0, b0 = split_weights(w_query, w_kv)
    a1, b1 = both_ways(a0, a0), both_ways(b0, b0)
    mine, *other = norm_split(layer_input, norm_gain.reshape(1, -1), places, core)
    theirs = [lax.ppermute(x, "pipe", CORE) for x in other]
    a2, b2 = both_ways(*a1), both_ways(*b1)
    a3 = both_ways(*a2)
    parts = ((0, BLK), (BLK, HD))
    pieces = [a0, b0, a1[0], b1[0], a1[1], b1[1]]
    accs = fwd_step(mine, theirs, ((0, 2), (1, 2), (2, 2)), pieces, parts)
    b2, accs = tie(b2, accs)
    b3 = both_ways(*b2)
    pieces = [a2[0], b2[0], a2[1], b2[1]]
    accs = fwd_step(mine, theirs, ((3, 2), (4, 2)), pieces, parts, accs)
    a3, accs = tie(a3, accs)
    a4 = both_ways(a3[0][:HD], a3[1][HD:])
    b4 = both_ways(b3[0][:HD], b3[1][HD:])
    pieces = [a3[0], b3[0], a3[1], b3[1], *a4, *b4]
    accs = fwd_step(mine, theirs, ((5, 2), (6, 2), (7, 4)), pieces, parts, accs)
    q, kv = exchange(accs[:2]), exchange(accs[2:])

    got_a = lax.ppermute(kv, "tensor", KV_OUT_A)
    got_b = lax.ppermute(kv, "tensor", KV_OUT_B)
    k = jnp.where(odd == 1, got_b, got_a)
    v = jnp.where(odd == 1, got_a, got_b)
    attn_out, gq, gk, gv = attention(bounds, q, k, v, out_grad)
    oth_q = lax.ppermute(gq, "pipe", CORE)
    split = 320
    act_a = gq[:split], oth_q[:split]
    step_a = grad("first", (4,), act_a)
    gk, gv, step_a = tie(gk, gv, step_a)
    got = lax.ppermute(jnp.where(odd == 1, gk, gv), "tensor", PAIR)
    gkv = (jnp.where(odd == 1, gv, gk) + got).astype(BF)
    step_a = both_ways(*step_a)
    gkv, step_a = tie(gkv, step_a)
    step_a = grad("second", (3, 5), act_a, step_a)
    step_a = both_ways(*step_a)
    own_kv = lax.ppermute(gkv, "tensor", KV_HOME)
    oth_kv = lax.ppermute(gkv, ("pipe", "tensor"), KV_ACROSS)
    act_b = (
        jnp.concatenate([gq[split:], own_kv], axis=0),
        jnp.concatenate([oth_q[split:], oth_kv], axis=0),
    )
    step_b = both_ways(*grad("first", (4,), act_b))
    step_a = both_ways(*grad("more", (2, 6), act_a, step_a))
    step_b = both_ways(*grad("second", (3, 5), act_b, step_b))
    step_a = both_ways(*grad("more", (1, 7), act_a, step_a))
    step_b = both_ways(*grad("more", (2, 6), act_b, step_b))
    step_b = both_ways(*grad("more", (1, 7), act_b, step_b))
    sums_a, sums_b = finish(act_a, step_a), finish(act_b, step_b)
    return attn_out, *join(*sums_a, *sums_b)


def solution(mesh):
    placed = (
        P(("pipe", "dp"), None),
        P(),
        P("pipe", "tensor"),
        P("pipe", "tensor"),
        P(("pipe", "dp"), None),
        P(("pipe", "dp"), "tensor"),
    )
    return jax.shard_map(
        local,
        mesh=mesh,
        in_specs=placed,
        out_specs=(
            P(("pipe", "dp"), "tensor"),
            P(("pipe", "dp"), "tensor"),
            P(("pipe", "dp"), "tensor"),
        ),
        check_vma=False,
    )
```

```python
import functools

import jax
import jax.numpy as jnp
from jax import lax
from jax.experimental import pallas as pl
from jax.experimental.pallas import tpu as pltpu
from jax.sharding import PartitionSpec as P

HEADS = 32
KV_HEADS = 4
HD = 128
RING = 8
BLK = 512
TOK = 512
HALF = BLK // 2
EACH = 4
PAIRED = 2
ORDER = (0, 7, 1, 6, 2, 5, 3, 4)
BF = jnp.bfloat16
F32 = jnp.float32


def ring_perm(step):
    return [(p, (p + 2 * step) % (2 * RING)) for p in range(2 * RING)]


CORE = [(p, p ^ 1) for p in range(2 * RING)]
DP = [(0, 1), (1, 0)]
VMEM = pl.BlockSpec(memory_space=pltpu.VMEM)
SMEM = pl.BlockSpec(memory_space=pltpu.SMEM)
COST = pl.CostEstimate(flops=1, bytes_accessed=1, transcendentals=0)
KV_OUT_A = [(g, 2 * g) for g in range(4)] + [(4 + g, 2 * g + 1) for g in range(4)]
KV_OUT_B = [(g, 2 * g + 1) for g in range(4)] + [(4 + g, 2 * g) for g in range(4)]
PAIR = [(t, t ^ 1) for t in range(8)]
KV_HOME = [(2 * g, g) for g in range(4)] + [(2 * g + 1, 4 + g) for g in range(4)]
KV_ACROSS = [(8 * p + t, 8 * (p ^ 1) + home) for p in range(16) for t, home in KV_HOME]


def params(mib=8):
    return pltpu.CompilerParams(vmem_limit_bytes=mib * 1024 * 1024)


def norm_body(place_ref, core_ref, x_ref, gain_ref, mine_ref, *other_refs):
    core = core_ref[0]
    rows = 32
    for start in range(0, x_ref.shape[0], rows):
        here = slice(start, start + rows)
        total = jnp.zeros((rows, HD), F32)
        for j in range(x_ref.shape[1] // HD):
            part = x_ref[here, j * HD : (j + 1) * HD].astype(F32)
            total = total + part * part
        mean = jnp.sum(total, axis=1, keepdims=True) / x_ref.shape[1]
        inv = lax.rsqrt(mean + 1e-05)
        for i in range(RING):
            for parity in (core, 1 - core):
                at = (2 * place_ref[i] + parity) * BLK
                cols = pl.ds(pl.multiple_of(at, BLK), BLK)
                part = x_ref[here, cols].astype(F32) * inv * gain_ref[:, cols]
                if parity is core:
                    mine_ref[i, here, :] = part.astype(BF)
                else:
                    other_refs[i // EACH][i % EACH, here, :] = part.astype(BF)


def norm_split(x, gain, places, core):
    rows = 128
    blocks = [RING] + [EACH] * (RING // EACH)
    return pl.pallas_call(
        norm_body,
        grid_spec=pltpu.PrefetchScalarGridSpec(
            num_scalar_prefetch=2,
            grid=(TOK // rows,),
            in_specs=[
                pl.BlockSpec((rows, 2 * RING * BLK), lambda i, s, t: (i, 0)),
                pl.BlockSpec((1, 2 * RING * BLK), lambda i, s, t: (0, 0)),
            ],
            out_specs=[pl.BlockSpec((n, rows, BLK), lambda i, s, t: (0, i, 0)) for n in blocks],
        ),
        out_shape=[jax.ShapeDtypeStruct((n, TOK, BLK), BF) for n in blocks],
        compiler_params=params(42),
        cost_estimate=COST,
        name="norm_split",
    )(places, core, x, gain)


def fwd_body(groups, parts, first, *refs):
    count = len(groups)
    pieces = sum(n for _, n in groups)
    own, oth, weights, rest = (
        refs[:count],
        refs[count : 2 * count],
        refs[2 * count : 2 * count + pieces],
        refs[2 * count + pieces :],
    )
    blocks = []
    for _, n in groups:
        rows = [w[...] for w in weights[:n]]
        blocks.append(jnp.concatenate(rows, axis=0) if n > 1 else rows[0])
        weights = weights[n:]
    for k, (start, wide) in enumerate(parts):
        for slot, xs in ((2 * k, own), (2 * k + 1, oth)):
            out_ref = rest[slot - 2 * len(parts)]
            out = jnp.zeros(out_ref.shape, F32) if first else rest[slot][...]
            for x, w in zip(xs, blocks, strict=True):
                w = w[:, start : start + wide]
                out = out + jnp.dot(x[0], w, preferred_element_type=F32)
            out_ref[...] = out


def fwd_step(mine, theirs, groups, weights, parts, accs=()):
    rows = 256

    def x_specs(each):
        return [
            pl.BlockSpec((1, rows, BLK), lambda i, at=at: (at % each, i, 0))
            for at, _ in groups
        ]

    w_specs = [pl.BlockSpec(w.shape, lambda i: (0, 0)) for w in weights]
    acc_specs = [
        pl.BlockSpec((rows, wide), lambda i: (i, 0)) for _, wide in parts for _ in "ab"
    ]
    return pl.pallas_call(
        functools.partial(fwd_body, groups, parts, not accs),
        grid=(TOK // rows,),
        in_specs=x_specs(RING) + x_specs(EACH) + w_specs + acc_specs[: len(accs)],
        out_specs=acc_specs,
        out_shape=[
            jax.ShapeDtypeStruct((TOK, wide), F32) for _, wide in parts for _ in "ab"
        ],
        compiler_params=params(20),
        cost_estimate=COST,
        name="fwd_step",
    )(
        *([mine] * len(groups)),
        *[theirs[at // EACH] for at, _ in groups],
        *weights,
        *accs,
    )


def attn_body(
    bounds_ref, q_ref, k_ref, v_ref, g_ref, o_ref, gq_ref, gk_ref, gv_ref, bias_ref
):
    scale = HD ** (-0.5)
    rows = 256
    nt = (((1,), (1,)), ((), ()))

    @pl.when(pl.program_id(0) == 0)
    def _():
        gk_ref[...] = jnp.zeros_like(gk_ref)
        gv_ref[...] = jnp.zeros_like(gv_ref)
        row = lax.broadcasted_iota(jnp.int32, (TOK, 1), 0)
        col = lax.broadcasted_iota(jnp.int32, (1, TOK), 1)
        start = jnp.zeros((TOK, 1), jnp.int32)
        for d in range(3):
            start = jnp.where(row >= bounds_ref[d], bounds_ref[d], start)
        bias_ref[...] = jnp.where((col <= row) & (col >= start), 0.0, -1e30)

    every = []
    for h in range(PAIRED):
        lanes = slice(h * HD, (h + 1) * HD)
        for i in range(TOK // rows):
            every.append((lanes, slice(i * rows, (i + 1) * rows), (i + 1) * rows))
    q = [q_ref[here, lanes] for lanes, here, _ in every]
    g = [g_ref[here, lanes] for lanes, here, _ in every]
    k = [k_ref[:n, :] for _, _, n in every]
    v = [v_ref[:n, :] for _, _, n in every]
    s = [lax.dot_general(x, y, nt, preferred_element_type=F32) for x, y in zip(q, k, strict=True)]
    b = [lax.dot_general(x, y, nt, preferred_element_type=F32) for x, y in zip(g, v, strict=True)]
    s = [x * scale + bias_ref[here, :n] for x, (_, here, n) in zip(s, every, strict=True)]
    e = [jnp.exp(x - jnp.max(x, axis=1, keepdims=True)) for x in s]
    p = [x * (1.0 / jnp.sum(x, axis=1, keepdims=True)) for x in e]
    delta = [jnp.sum(x * y, axis=1, keepdims=True) for x, y in zip(p, b, strict=True)]
    pb = [x.astype(BF) for x in p]
    sg = [
        (x * (y - d) * scale).astype(BF) for x, y, d in zip(p, b, delta, strict=True)
    ]
    for i, (lanes, here, _) in enumerate(every):
        o_ref[here, lanes] = jnp.dot(pb[i], v[i], preferred_element_type=F32).astype(BF)
        gq = jnp.dot(sg[i], k[i], preferred_element_type=F32)
        gq_ref[lanes, here] = gq.T.astype(BF)
    gk = [jnp.dot(x.T, y, preferred_element_type=F32) for x, y in zip(q, sg, strict=True)]
    gv = [jnp.dot(x.T, y, preferred_element_type=F32) for x, y in zip(g, pb, strict=True)]
    for ref, terms in ((gk_ref, gk), (gv_ref, gv)):
        low, high = sum(terms[2::2], terms[0]), sum(terms[3::2], terms[1])
        ref[:, :rows] += low + high[:, :rows]
        ref[:, rows:] += high[:, rows:]


def attention(bounds, q, k, v, out_grad):
    heads = out_grad.shape[1] // HD
    out = jax.ShapeDtypeStruct((TOK, heads * HD), BF)
    grad = jax.ShapeDtypeStruct((heads * HD, TOK), BF)
    kv_out = jax.ShapeDtypeStruct((HD, TOK), F32)
    whole = pl.BlockSpec((TOK, HD), lambda h, s: (0, 0))
    whole_t = pl.BlockSpec((HD, TOK), lambda h, s: (0, 0))
    return pl.pallas_call(
        attn_body,
        grid_spec=pltpu.PrefetchScalarGridSpec(
            num_scalar_prefetch=1,
            grid=(heads // PAIRED,),
            in_specs=[
                pl.BlockSpec((TOK, PAIRED * HD), lambda h, s: (0, h)),
                whole,
                whole,
                pl.BlockSpec((TOK, PAIRED * HD), lambda h, s: (0, h)),
            ],
            out_specs=[
                pl.BlockSpec((TOK, PAIRED * HD), lambda h, s: (0, h)),
                pl.BlockSpec((PAIRED * HD, TOK), lambda h, s: (h, 0)),
                whole_t,
                whole_t,
            ],
            scratch_shapes=[pltpu.VMEM((TOK, TOK), F32)],
        ),
        out_shape=[out, grad, kv_out, kv_out],
        compiler_params=params(20),
        cost_estimate=COST,
        name="attention",
    )(bounds, q, k, v, out_grad)


def grad_body(kind, *refs):
    count = 2 if kind in ("second", "more") else 1
    xs, (own_ref, oth_ref), rest = refs[: 2 * count], refs[2 * count :][:2], refs[2 * count + 2 :]
    for i in range(count):
        g = jnp.dot(own_ref[...], xs[2 * i][0], preferred_element_type=F32)
        g += jnp.dot(oth_ref[...], xs[2 * i + 1][0], preferred_element_type=F32)
        if kind == "first":
            rest[0][...] = g[:, :HALF].astype(BF)
            rest[1][...] = g[:, HALF:].astype(BF)
        elif kind == "second":
            got, out = rest[i], rest[2 + i]
            hit = slice(i * HALF, (i + 1) * HALF)
            miss = slice((1 - i) * HALF, (2 - i) * HALF)
            out[:, hit] = (g[:, hit] + got[...].astype(F32)).astype(BF)
            out[:, miss] = g[:, miss].astype(BF)
        elif kind == "more":
            rest[2 + i][...] = (g + rest[i][...].astype(F32)).astype(BF)
        else:
            g = g + rest[0][...].astype(F32) + rest[1][...].astype(F32)
            low = rest[2][0] == 0
            rest[3][...] = jnp.where(low, g[:, :HALF], g[:, HALF:])
            rest[4][...] = jnp.where(low, g[:, HALF:], g[:, :HALF]).astype(BF)


def grad_step(kind, mine, theirs, blocks, a_own, a_oth, got=(), side=()):
    cols = a_own.shape[0]
    rows = cols // 2
    xs, x_specs = [], []
    for at in blocks:
        for x, j in ((mine, at), (theirs[at // EACH], at % EACH)):
            xs.append(x)
            x_specs.append(pl.BlockSpec((1, TOK, BLK), lambda i, j=j: (j, 0, 0)))
    a_spec = pl.BlockSpec((rows, TOK), lambda i: (i, 0))
    if kind == "last":
        outs = [jax.ShapeDtypeStruct((cols, HALF), dtype) for dtype in (F32, BF)]
    else:
        wide = HALF if kind == "first" else BLK
        outs = [jax.ShapeDtypeStruct((cols, wide), BF)] * 2

    def row_spec(x):
        return pl.BlockSpec((rows, x.shape[1]), lambda i: (i, 0))

    return pl.pallas_call(
        functools.partial(grad_body, kind),
        grid=(cols // rows,),
        in_specs=x_specs
        + [a_spec, a_spec]
        + [row_spec(x) for x in got]
        + [SMEM for _ in side],
        out_specs=[row_spec(x) for x in outs],
        out_shape=outs,
        compiler_params=params(16),
        cost_estimate=COST,
        name="grad_step",
    )(*xs, a_own, a_oth, *got, *side)


def join_body(a_ref, a_got_ref, b_ref, b_got_ref, q_ref, kv_ref):
    a = (a_ref[...] + a_got_ref[...].astype(F32)).T
    b = (b_ref[...] + b_got_ref[...].astype(F32)).T
    both = jnp.concatenate([a, b], axis=1)
    q_ref[...] = both[:, :BLK]
    kv_ref[...] = both[:, BLK:]


def join(*sums):
    return pl.pallas_call(
        join_body,
        out_shape=[
            jax.ShapeDtypeStruct((HALF, BLK), F32),
            jax.ShapeDtypeStruct((HALF, HD), F32),
        ],
        compiler_params=params(16),
        cost_estimate=COST,
        name="join",
    )(*sums)


def split_body(q_ref, kv_ref, a_ref, b_ref):
    for rows, out in ((slice(0, HALF), a_ref), (slice(HALF, BLK), b_ref)):
        out[:, :BLK] = q_ref[rows, :]
        out[:, BLK:] = kv_ref[rows, :]


def split_weights(w_query, w_kv):
    out = jax.ShapeDtypeStruct((HALF, BLK + HD), BF)
    return pl.pallas_call(
        split_body,
        out_shape=[out, out],
        compiler_params=params(),
        cost_estimate=COST,
        name="split_weights",
    )(w_query, w_kv)


def both_ways(f, b):
    f = lax.ppermute(f, "pipe", ring_perm(1))
    b = lax.ppermute(b, "pipe", ring_perm(-1))
    return lax.optimization_barrier((f, b))


def local(layer_input, norm_gain, w_query, w_kv, lengths, out_grad):
    pipe = lax.axis_index("pipe")
    z, core = pipe // 2, (pipe % 2).reshape(1)
    odd = lax.axis_index("tensor") % 2
    dp = lax.axis_index("dp")
    bounds = jnp.cumsum(lengths[0])[:3].astype(jnp.int32)

    def exchange(accs):
        return (accs[0] + lax.ppermute(accs[1], "pipe", CORE)).astype(BF)

    def grad(kind, offsets, own_oth, got=(), side=()):
        blocks = [ORDER.index(offset) for offset in offsets]
        return grad_step(kind, mine, theirs, blocks, *own_oth, got, side)

    def finish(own_oth, got):
        keep, give = grad("last", (0,), own_oth, got, (dp.reshape(1),))
        return keep, lax.ppermute(give, "dp", DP)

    def tie(*values):
        return lax.optimization_barrier(values)

    places = (z + jnp.array(ORDER, jnp.int32)) % RING
    a0, b0 = split_weights(w_query, w_kv)
    a1, b1 = both_ways(a0, a0), both_ways(b0, b0)
    mine, *other = norm_split(layer_input, norm_gain.reshape(1, -1), places, core)
    theirs = [lax.ppermute(x, "pipe", CORE) for x in other]
    a2, b2 = both_ways(*a1), both_ways(*b1)
    a3 = both_ways(*a2)
    parts = ((0, BLK), (BLK, HD))
    pieces = [a0, b0, a1[0], b1[0], a1[1], b1[1]]
    accs = fwd_step(mine, theirs, ((0, 2), (1, 2), (2, 2)), pieces, parts)
    b2, accs = tie(b2, accs)
    b3 = both_ways(*b2)
    pieces = [a2[0], b2[0], a2[1], b2[1]]
    accs = fwd_step(mine, theirs, ((3, 2), (4, 2)), pieces, parts, accs)
    a3, accs = tie(a3, accs)
    a4 = both_ways(a3[0][:HD], a3[1][HD:])
    b4 = both_ways(b3[0][:HD], b3[1][HD:])
    pieces = [a3[0], b3[0], a3[1], b3[1], *a4, *b4]
    accs = fwd_step(mine, theirs, ((5, 2), (6, 2), (7, 4)), pieces, parts, accs)
    q, kv = exchange(accs[:2]), exchange(accs[2:])

    got_a = lax.ppermute(kv, "tensor", KV_OUT_A)
    got_b = lax.ppermute(kv, "tensor", KV_OUT_B)
    k = jnp.where(odd == 1, got_b, got_a)
    v = jnp.where(odd == 1, got_a, got_b)
    attn_out, gq, gk, gv = attention(bounds, q, k, v, out_grad)
    oth_q = lax.ppermute(gq, "pipe", CORE)
    split = 320
    act_a = gq[:split], oth_q[:split]
    step_a = grad("first", (4,), act_a)
    gk, gv, step_a = tie(gk, gv, step_a)
    got = lax.ppermute(jnp.where(odd == 1, gk, gv), "tensor", PAIR)
    gkv = (jnp.where(odd == 1, gv, gk) + got).astype(BF)
    step_a = both_ways(*step_a)
    gkv, step_a = tie(gkv, step_a)
    step_a = grad("second", (3, 5), act_a, step_a)
    step_a = both_ways(*step_a)
    own_kv = lax.ppermute(gkv, "tensor", KV_HOME)
    oth_kv = lax.ppermute(gkv, ("pipe", "tensor"), KV_ACROSS)
    act_b = (
        jnp.concatenate([gq[split:], own_kv], axis=0),
        jnp.concatenate([oth_q[split:], oth_kv], axis=0),
    )
    step_b = both_ways(*grad("first", (4,), act_b))
    step_a = both_ways(*grad("more", (2, 6), act_a, step_a))
    step_b = both_ways(*grad("second", (3, 5), act_b, step_b))
    step_a = both_ways(*grad("more", (1, 7), act_a, step_a))
    step_b = both_ways(*grad("more", (2, 6), act_b, step_b))
    step_b = both_ways(*grad("more", (1, 7), act_b, step_b))
    sums_a, sums_b = finish(act_a, step_a), finish(act_b, step_b)
    return attn_out, *join(*sums_a, *sums_b)


def solution(mesh):
    placed = (
        P(("pipe", "dp"), None),
        P(),
        P("pipe", "tensor"),
        P("pipe", "tensor"),
        P(("pipe", "dp"), None),
        P(("pipe", "dp"), "tensor"),
    )
    return jax.shard_map(
        local,
        mesh=mesh,
        in_specs=placed,
        out_specs=(
            P(("pipe", "dp"), "tensor"),
            P(("pipe", "dp"), "tensor"),
            P(("pipe", "dp"), "tensor"),
        ),
        check_vma=False,
    )
```

```python
import functools

import jax
import jax.numpy as jnp
from jax import lax
from jax.experimental import pallas as pl
from jax.experimental.pallas import tpu as pltpu
from jax.sharding import PartitionSpec as P

HEADS = 32
KV_HEADS = 4
HD = 128
RING = 8
BLK = 512
TOK = 512
HALF = BLK // 2
EACH = 4
PAIRED = 2
ORDER = (0, 7, 1, 6, 2, 5, 3, 4)
BF = jnp.bfloat16
F32 = jnp.float32


def ring_perm(step):
    return [(p, (p + 2 * step) % (2 * RING)) for p in range(2 * RING)]


CORE = [(p, p ^ 1) for p in range(2 * RING)]
DP = [(0, 1), (1, 0)]
VMEM = pl.BlockSpec(memory_space=pltpu.VMEM)
SMEM = pl.BlockSpec(memory_space=pltpu.SMEM)
COST = pl.CostEstimate(flops=1, bytes_accessed=1, transcendentals=0)
KV_OUT_A = [(g, 2 * g) for g in range(4)] + [(4 + g, 2 * g + 1) for g in range(4)]
KV_OUT_B = [(g, 2 * g + 1) for g in range(4)] + [(4 + g, 2 * g) for g in range(4)]
PAIR = [(t, t ^ 1) for t in range(8)]
KV_HOME = [(2 * g, g) for g in range(4)] + [(2 * g + 1, 4 + g) for g in range(4)]
KV_ACROSS = [(8 * p + t, 8 * (p ^ 1) + home) for p in range(16) for t, home in KV_HOME]


def params(mib=8):
    return pltpu.CompilerParams(vmem_limit_bytes=mib * 1024 * 1024)


def norm_body(place_ref, core_ref, x_ref, gain_ref, mine_ref, *other_refs):
    core = core_ref[0]
    rows = 32
    for start in range(0, x_ref.shape[0], rows):
        here = slice(start, start + rows)
        total = jnp.zeros((rows, HD), F32)
        for j in range(x_ref.shape[1] // HD):
            part = x_ref[here, j * HD : (j + 1) * HD].astype(F32)
            total = total + part * part
        mean = jnp.sum(total, axis=1, keepdims=True) / x_ref.shape[1]
        inv = lax.rsqrt(mean + 1e-05)
        for i in range(RING):
            for parity in (core, 1 - core):
                at = (2 * place_ref[i] + parity) * BLK
                cols = pl.ds(pl.multiple_of(at, BLK), BLK)
                part = x_ref[here, cols].astype(F32) * inv * gain_ref[:, cols]
                if parity is core:
                    mine_ref[i, here, :] = part.astype(BF)
                else:
                    other_refs[i // EACH][i % EACH, here, :] = part.astype(BF)


def norm_split(x, gain, places, core):
    rows = 128
    blocks = [RING] + [EACH] * (RING // EACH)
    return pl.pallas_call(
        norm_body,
        grid_spec=pltpu.PrefetchScalarGridSpec(
            num_scalar_prefetch=2,
            grid=(TOK // rows,),
            in_specs=[
                pl.BlockSpec((rows, 2 * RING * BLK), lambda i, s, t: (i, 0)),
                pl.BlockSpec((1, 2 * RING * BLK), lambda i, s, t: (0, 0)),
            ],
            out_specs=[pl.BlockSpec((n, rows, BLK), lambda i, s, t: (0, i, 0)) for n in blocks],
        ),
        out_shape=[jax.ShapeDtypeStruct((n, TOK, BLK), BF) for n in blocks],
        compiler_params=params(42),
        cost_estimate=COST,
        name="norm_split",
    )(places, core, x, gain)


def fwd_body(groups, parts, first, *refs):
    count = len(groups)
    pieces = sum(n for _, n in groups)
    own, oth, weights, rest = (
        refs[:count],
        refs[count : 2 * count],
        refs[2 * count : 2 * count + pieces],
        refs[2 * count + pieces :],
    )
    blocks = []
    for _, n in groups:
        rows = [w[...] for w in weights[:n]]
        blocks.append(jnp.concatenate(rows, axis=0) if n > 1 else rows[0])
        weights = weights[n:]
    for k, (start, wide) in enumerate(parts):
        for slot, xs in ((2 * k, own), (2 * k + 1, oth)):
            out_ref = rest[slot - 2 * len(parts)]
            out = jnp.zeros(out_ref.shape, F32) if first else rest[slot][...]
            for x, w in zip(xs, blocks, strict=True):
                w = w[:, start : start + wide]
                out = out + jnp.dot(x[0], w, preferred_element_type=F32)
            out_ref[...] = out


def fwd_step(mine, theirs, groups, weights, parts, accs=()):
    rows = 256

    def x_specs(each):
        return [
            pl.BlockSpec((1, rows, BLK), lambda i, at=at: (at % each, i, 0))
            for at, _ in groups
        ]

    w_specs = [pl.BlockSpec(w.shape, lambda i: (0, 0)) for w in weights]
    acc_specs = [
        pl.BlockSpec((rows, wide), lambda i: (i, 0)) for _, wide in parts for _ in "ab"
    ]
    return pl.pallas_call(
        functools.partial(fwd_body, groups, parts, not accs),
        grid=(TOK // rows,),
        in_specs=x_specs(RING) + x_specs(EACH) + w_specs + acc_specs[: len(accs)],
        out_specs=acc_specs,
        out_shape=[
            jax.ShapeDtypeStruct((TOK, wide), F32) for _, wide in parts for _ in "ab"
        ],
        compiler_params=params(20),
        cost_estimate=COST,
        name="fwd_step",
    )(
        *([mine] * len(groups)),
        *[theirs[at // EACH] for at, _ in groups],
        *weights,
        *accs,
    )


def attn_body(
    bounds_ref, q_ref, k_ref, v_ref, g_ref, o_ref, gq_ref, gk_ref, gv_ref, bias_ref
):
    scale = HD ** (-0.5)
    rows = 256
    nt = (((1,), (1,)), ((), ()))

    @pl.when(pl.program_id(0) == 0)
    def _():
        gk_ref[...] = jnp.zeros_like(gk_ref)
        gv_ref[...] = jnp.zeros_like(gv_ref)
        row = lax.broadcasted_iota(jnp.int32, (TOK, 1), 0)
        col = lax.broadcasted_iota(jnp.int32, (1, TOK), 1)
        start = jnp.zeros((TOK, 1), jnp.int32)
        for d in range(3):
            start = jnp.where(row >= bounds_ref[d], bounds_ref[d], start)
        bias_ref[...] = jnp.where((col <= row) & (col >= start), 0.0, -1e30)

    every = []
    for h in range(PAIRED):
        lanes = slice(h * HD, (h + 1) * HD)
        for i in range(TOK // rows):
            every.append((lanes, slice(i * rows, (i + 1) * rows), (i + 1) * rows))
    q = [q_ref[here, lanes] for lanes, here, _ in every]
    g = [g_ref[here, lanes] for lanes, here, _ in every]
    k = [k_ref[:n, :] for _, _, n in every]
    v = [v_ref[:n, :] for _, _, n in every]
    s = [lax.dot_general(x, y, nt, preferred_element_type=F32) for x, y in zip(q, k, strict=True)]
    b = [lax.dot_general(x, y, nt, preferred_element_type=F32) for x, y in zip(g, v, strict=True)]
    s = [x * scale + bias_ref[here, :n] for x, (_, here, n) in zip(s, every, strict=True)]
    e = [jnp.exp(x - jnp.max(x, axis=1, keepdims=True)) for x in s]
    p = [x * (1.0 / jnp.sum(x, axis=1, keepdims=True)) for x in e]
    delta = [jnp.sum(x * y, axis=1, keepdims=True) for x, y in zip(p, b, strict=True)]
    pb = [x.astype(BF) for x in p]
    sg = [
        (x * (y - d) * scale).astype(BF) for x, y, d in zip(p, b, delta, strict=True)
    ]
    for i, (lanes, here, _) in enumerate(every):
        o_ref[here, lanes] = jnp.dot(pb[i], v[i], preferred_element_type=F32).astype(BF)
        gq = jnp.dot(sg[i], k[i], preferred_element_type=F32)
        gq_ref[lanes, here] = gq.T.astype(BF)
    gk = [jnp.dot(x.T, y, preferred_element_type=F32) for x, y in zip(q, sg, strict=True)]
    gv = [jnp.dot(x.T, y, preferred_element_type=F32) for x, y in zip(g, pb, strict=True)]
    for ref, terms in ((gk_ref, gk), (gv_ref, gv)):
        low, high = sum(terms[2::2], terms[0]), sum(terms[3::2], terms[1])
        ref[:, :rows] += low + high[:, :rows]
        ref[:, rows:] += high[:, rows:]


def attention(bounds, q, k, v, out_grad):
    heads = out_grad.shape[1] // HD
    out = jax.ShapeDtypeStruct((TOK, heads * HD), BF)
    grad = jax.ShapeDtypeStruct((heads * HD, TOK), BF)
    kv_out = jax.ShapeDtypeStruct((HD, TOK), F32)
    whole = pl.BlockSpec((TOK, HD), lambda h, s: (0, 0))
    whole_t = pl.BlockSpec((HD, TOK), lambda h, s: (0, 0))
    return pl.pallas_call(
        attn_body,
        grid_spec=pltpu.PrefetchScalarGridSpec(
            num_scalar_prefetch=1,
            grid=(heads // PAIRED,),
            in_specs=[
                pl.BlockSpec((TOK, PAIRED * HD), lambda h, s: (0, h)),
                whole,
                whole,
                pl.BlockSpec((TOK, PAIRED * HD), lambda h, s: (0, h)),
            ],
            out_specs=[
                pl.BlockSpec((TOK, PAIRED * HD), lambda h, s: (0, h)),
                pl.BlockSpec((PAIRED * HD, TOK), lambda h, s: (h, 0)),
                whole_t,
                whole_t,
            ],
            scratch_shapes=[pltpu.VMEM((TOK, TOK), F32)],
        ),
        out_shape=[out, grad, kv_out, kv_out],
        compiler_params=params(20),
        cost_estimate=COST,
        name="attention",
    )(bounds, q, k, v, out_grad)


def grad_body(kind, *refs):
    count = 2 if kind in ("second", "more") else 1
    xs, (own_ref, oth_ref), rest = refs[: 2 * count], refs[2 * count :][:2], refs[2 * count + 2 :]
    for i in range(count):
        g = jnp.dot(own_ref[...], xs[2 * i][0], preferred_element_type=F32)
        g += jnp.dot(oth_ref[...], xs[2 * i + 1][0], preferred_element_type=F32)
        if kind == "first":
            rest[0][...] = g[:, :HALF].astype(BF)
            rest[1][...] = g[:, HALF:].astype(BF)
        elif kind == "second":
            got, out = rest[i], rest[2 + i]
            hit = slice(i * HALF, (i + 1) * HALF)
            miss = slice((1 - i) * HALF, (2 - i) * HALF)
            out[:, hit] = (g[:, hit] + got[...].astype(F32)).astype(BF)
            out[:, miss] = g[:, miss].astype(BF)
        elif kind == "more":
            rest[2 + i][...] = (g + rest[i][...].astype(F32)).astype(BF)
        else:
            g = g + rest[0][...].astype(F32) + rest[1][...].astype(F32)
            low = rest[2][0] == 0
            rest[3][...] = jnp.where(low, g[:, :HALF], g[:, HALF:])
            rest[4][...] = jnp.where(low, g[:, HALF:], g[:, :HALF]).astype(BF)


def grad_step(kind, mine, theirs, blocks, a_own, a_oth, got=(), side=()):
    cols = a_own.shape[0]
    rows = cols
    xs, x_specs = [], []
    for at in blocks:
        for x, j in ((mine, at), (theirs[at // EACH], at % EACH)):
            xs.append(x)
            x_specs.append(pl.BlockSpec((1, TOK, BLK), lambda i, j=j: (j, 0, 0)))
    a_spec = pl.BlockSpec((rows, TOK), lambda i: (i, 0))
    if kind == "last":
        outs = [jax.ShapeDtypeStruct((cols, HALF), dtype) for dtype in (F32, BF)]
    else:
        wide = HALF if kind == "first" else BLK
        outs = [jax.ShapeDtypeStruct((cols, wide), BF)] * 2

    def row_spec(x):
        return pl.BlockSpec((rows, x.shape[1]), lambda i: (i, 0))

    return pl.pallas_call(
        functools.partial(grad_body, kind),
        grid=(cols // rows,),
        in_specs=x_specs
        + [a_spec, a_spec]
        + [row_spec(x) for x in got]
        + [SMEM for _ in side],
        out_specs=[row_spec(x) for x in outs],
        out_shape=outs,
        compiler_params=params(16),
        cost_estimate=COST,
        name="grad_step",
    )(*xs, a_own, a_oth, *got, *side)


def join_body(a_ref, a_got_ref, b_ref, b_got_ref, q_ref, kv_ref):
    a = (a_ref[...] + a_got_ref[...].astype(F32)).T
    b = (b_ref[...] + b_got_ref[...].astype(F32)).T
    both = jnp.concatenate([a, b], axis=1)
    q_ref[...] = both[:, :BLK]
    kv_ref[...] = both[:, BLK:]


def join(*sums):
    return pl.pallas_call(
        join_body,
        out_shape=[
            jax.ShapeDtypeStruct((HALF, BLK), F32),
            jax.ShapeDtypeStruct((HALF, HD), F32),
        ],
        compiler_params=params(16),
        cost_estimate=COST,
        name="join",
    )(*sums)


def split_body(q_ref, kv_ref, a_ref, b_ref):
    for rows, out in ((slice(0, HALF), a_ref), (slice(HALF, BLK), b_ref)):
        out[:, :BLK] = q_ref[rows, :]
        out[:, BLK:] = kv_ref[rows, :]


def split_weights(w_query, w_kv):
    out = jax.ShapeDtypeStruct((HALF, BLK + HD), BF)
    return pl.pallas_call(
        split_body,
        out_shape=[out, out],
        compiler_params=params(),
        cost_estimate=COST,
        name="split_weights",
    )(w_query, w_kv)


def both_ways(f, b):
    f = lax.ppermute(f, "pipe", ring_perm(1))
    b = lax.ppermute(b, "pipe", ring_perm(-1))
    return lax.optimization_barrier((f, b))


def local(layer_input, norm_gain, w_query, w_kv, lengths, out_grad):
    pipe = lax.axis_index("pipe")
    z, core = pipe // 2, (pipe % 2).reshape(1)
    odd = lax.axis_index("tensor") % 2
    dp = lax.axis_index("dp")
    bounds = jnp.cumsum(lengths[0])[:3].astype(jnp.int32)

    def exchange(accs):
        return (accs[0] + lax.ppermute(accs[1], "pipe", CORE)).astype(BF)

    def grad(kind, offsets, own_oth, got=(), side=()):
        blocks = [ORDER.index(offset) for offset in offsets]
        return grad_step(kind, mine, theirs, blocks, *own_oth, got, side)

    def finish(own_oth, got):
        keep, give = grad("last", (0,), own_oth, got, (dp.reshape(1),))
        return keep, lax.ppermute(give, "dp", DP)

    def tie(*values):
        return lax.optimization_barrier(values)

    places = (z + jnp.array(ORDER, jnp.int32)) % RING
    a0, b0 = split_weights(w_query, w_kv)
    a1, b1 = both_ways(a0, a0), both_ways(b0, b0)
    mine, *other = norm_split(layer_input, norm_gain.reshape(1, -1), places, core)
    theirs = [lax.ppermute(x, "pipe", CORE) for x in other]
    a2, b2 = both_ways(*a1), both_ways(*b1)
    a3 = both_ways(*a2)
    parts = ((0, BLK), (BLK, HD))
    pieces = [a0, b0, a1[0], b1[0], a1[1], b1[1]]
    accs = fwd_step(mine, theirs, ((0, 2), (1, 2), (2, 2)), pieces, parts)
    b2, accs = tie(b2, accs)
    b3 = both_ways(*b2)
    pieces = [a2[0], b2[0], a2[1], b2[1]]
    accs = fwd_step(mine, theirs, ((3, 2), (4, 2)), pieces, parts, accs)
    a3, accs = tie(a3, accs)
    a4 = both_ways(a3[0][:HD], a3[1][HD:])
    b4 = both_ways(b3[0][:HD], b3[1][HD:])
    pieces = [a3[0], b3[0], a3[1], b3[1], *a4, *b4]
    accs = fwd_step(mine, theirs, ((5, 2), (6, 2), (7, 4)), pieces, parts, accs)
    q, kv = exchange(accs[:2]), exchange(accs[2:])

    got_a = lax.ppermute(kv, "tensor", KV_OUT_A)
    got_b = lax.ppermute(kv, "tensor", KV_OUT_B)
    k = jnp.where(odd == 1, got_b, got_a)
    v = jnp.where(odd == 1, got_a, got_b)
    attn_out, gq, gk, gv = attention(bounds, q, k, v, out_grad)
    oth_q = lax.ppermute(gq, "pipe", CORE)
    split = 320
    act_a = gq[:split], oth_q[:split]
    step_a = grad("first", (4,), act_a)
    gk, gv, step_a = tie(gk, gv, step_a)
    got = lax.ppermute(jnp.where(odd == 1, gk, gv), "tensor", PAIR)
    gkv = (jnp.where(odd == 1, gv, gk) + got).astype(BF)
    step_a = both_ways(*step_a)
    gkv, step_a = tie(gkv, step_a)
    step_a = grad("second", (3, 5), act_a, step_a)
    step_a = both_ways(*step_a)
    own_kv = lax.ppermute(gkv, "tensor", KV_HOME)
    oth_kv = lax.ppermute(gkv, ("pipe", "tensor"), KV_ACROSS)
    act_b = (
        jnp.concatenate([gq[split:], own_kv], axis=0),
        jnp.concatenate([oth_q[split:], oth_kv], axis=0),
    )
    step_b = both_ways(*grad("first", (4,), act_b))
    step_a = both_ways(*grad("more", (2, 6), act_a, step_a))
    step_b = both_ways(*grad("second", (3, 5), act_b, step_b))
    step_a = both_ways(*grad("more", (1, 7), act_a, step_a))
    step_b = both_ways(*grad("more", (2, 6), act_b, step_b))
    step_b = both_ways(*grad("more", (1, 7), act_b, step_b))
    sums_a, sums_b = finish(act_a, step_a), finish(act_b, step_b)
    return attn_out, *join(*sums_a, *sums_b)


def solution(mesh):
    placed = (
        P(("pipe", "dp"), None),
        P(),
        P("pipe", "tensor"),
        P("pipe", "tensor"),
        P(("pipe", "dp"), None),
        P(("pipe", "dp"), "tensor"),
    )
    return jax.shard_map(
        local,
        mesh=mesh,
        in_specs=placed,
        out_specs=(
            P(("pipe", "dp"), "tensor"),
            P(("pipe", "dp"), "tensor"),
            P(("pipe", "dp"), "tensor"),
        ),
        check_vma=False,
    )
```
